128 devices in a mesh: gx: 16 (over y, z), gy: 8 (over x, core).
Axes of the slice: x: 4, y: 4, z: 4, core: 2. Of those that a mesh axis runs over, the one named last changes fastest.
Arguments:
- points: float32 [65536, 768], P(('gx', 'gy'))
- labels: float32 [65536, 64], P(('gx', 'gy')), may hold values from -16 to 16
- skeleton_rows: int32 [128, 256], P(('gx', 'gy')), may hold values from 0 to 511, as said below
- upper_rows: int32 [16, 256], P('gx'), may hold values from 0 to 2047, as said below
- near_list: int32 [256, 8], P(('gx', 'gy')), may hold values from 0 to 255, as said below
- far_local: int32 [128, 7], P(('gx', 'gy')), may hold values from -1 to 7, as said below
- far_upper: int32 [128, 15], P(('gx', 'gy')), may hold values from -1 to 15, as said below
Outputs:
- propagated: float32 [65536, 64], P(('gx', 'gy'))
The draws below stay inside these ranges and needn't reach their ends.
Inputs may be any that keep to these rules, and one draw needn't show every extreme that they name: `skeleton_rows`: entries of one row are distinct. `upper_rows`: entries of one row are distinct. `near_list`: row l lists distinct leaves of l's own outer cluster; its first entry is l itself. `far_local`: row g lists distinct node numbers within g's outer cluster (0 to 7), never g's own, first, then -1 in the remaining slots; at least one entry; some node lists all 7 others. `far_upper`: row g lists distinct outer clusters, never g's own, first, then -1 in the remaining slots; at least one entry; some node lists all 15 others.
All inputs are finite; a program needn't handle non-finite values.
Results may differ from the reference program's by a relative error of at most 0.0003.
Values sent between devices are 32-bit elements; how exact they have to be, the bound alone decides.
A program may use at most 128 MiB of HBM per device.

```python
import math
import jax
import jax.numpy as jnp
from jax import lax

D = 768
C = 64
LEAF = 256
SKEL = 256
NEAR = 8
LEAF_DEV = 2
GROUPS = 16
SUBNODES = 8
NODES = 128
LEAVES = 256
POINTS = 65536


def draw_points(key, part):
    key = jax.random.fold_in(key, 1)
    keys = jax.random.split(key, 4)
    shapes = [(POINTS, D), (LEAVES, D), (NODES, D), (GROUPS, D)]
    pieces = [jax.random.normal(keys[position], shapes[position], jnp.float32) / math.sqrt(D) for position in range(4)]
    squares = (0.5, 0.01, 0.01, 0.02)
    noise, leaf_centre, node_centre, group_centre = pieces
    result = math.sqrt(squares[0]) * noise.reshape(LEAVES, LEAF, D) + math.sqrt(squares[1]) * leaf_centre[:, None, :]
    result = result + math.sqrt(squares[2]) * jnp.repeat(node_centre, LEAF_DEV, axis=0)[:, None, :]
    result = result + math.sqrt(squares[3]) * jnp.repeat(group_centre, SUBNODES * LEAF_DEV, axis=0)[:, None, :]
    return result.reshape(POINTS, D)


def pick_rows(key, row_total, population, taken):
    keys = jax.random.split(key, row_total)
    return jax.vmap(lambda single: jax.random.permutation(single, population)[:taken])(keys).astype(jnp.int32)


def draw_skeleton_rows(key, part):
    key = jax.random.fold_in(key, 2)
    return pick_rows(key, NODES, LEAF_DEV * LEAF, SKEL)


def draw_upper_rows(key, part):
    key = jax.random.fold_in(key, 3)
    return pick_rows(key, GROUPS, SUBNODES * SKEL, SKEL)


def draw_near_list(key, part):
    key = jax.random.fold_in(key, 4)
    group_leaves = SUBNODES * LEAF_DEV
    keys = jax.random.split(key, LEAVES)

    def one_leaf(single, leaf_index):
        local = leaf_index % group_leaves
        others = jax.random.permutation(single, group_leaves - 1)[:NEAR - 1].astype(jnp.int32)
        others = others + (others >= local).astype(jnp.int32)
        return jnp.concatenate([leaf_index[None], leaf_index - local + others]).astype(jnp.int32)
    return jax.vmap(one_leaf)(keys, jnp.arange(LEAVES, dtype=jnp.int32))


def ragged_lists(key, row_total, width, owners):
    keys = jax.random.split(key, row_total + 2)
    spread_draw = jax.random.randint(keys[0], (row_total,), 0, width - 1)
    lengths = 1 + spread_draw * spread_draw // (width - 1)
    full_row = jax.random.randint(keys[1], (), 0, row_total)
    lengths = jnp.where(jnp.arange(row_total) == full_row, width - 1, lengths)

    def one_row(single, owner, length):
        order = jax.random.permutation(single, width - 1).astype(jnp.int32)
        order = order + (order >= owner).astype(jnp.int32)
        return jnp.where(jnp.arange(width - 1) < length, order, -1).astype(jnp.int32)
    return jax.vmap(one_row)(keys[2:], owners, lengths)


def draw_far_local(key, part):
    key = jax.random.fold_in(key, 5)
    owners = jnp.arange(NODES, dtype=jnp.int32) % SUBNODES
    return ragged_lists(key, NODES, SUBNODES, owners)


def draw_far_upper(key, part):
    key = jax.random.fold_in(key, 6)
    owners = jnp.arange(NODES, dtype=jnp.int32) // SUBNODES
    return ragged_lists(key, NODES, GROUPS, owners)


def levels(key, shape, cuts, low, top_value):
    level = 1.0
    for axis_at, shards_of in cuts:
        heights = jax.random.uniform(jax.random.fold_in(jax.random.fold_in(key, 6), axis_at), (shards_of,), jnp.float32, low / len(cuts), top_value / len(cuts))
        level = level * jnp.repeat(jnp.exp(heights), shape[axis_at] // shards_of).reshape((-1,) + (1,) * (len(shape) - 1 - axis_at))
    return level


def gaussian(own_key, extent, deviation, bound, cuts=(), held_as=jnp.bfloat16):
    values = deviation * jax.random.normal(own_key, extent, jnp.float32)
    if cuts:
        values = values * levels(own_key, extent, cuts, -0.22, 0.18)
    return jnp.clip(values, -bound, bound).astype(held_as)


def setup_inputs(seed: int = 0) -> dict:
    splits = jax.random.split(jax.random.key(seed), 8)
    points = draw_points(jax.random.fold_in(splits[7], 71), 0)
    labels = gaussian(splits[1], (POINTS, C), 4.0, 16.0, ((0, 128),), jnp.float32)
    skeleton_rows = draw_skeleton_rows(jax.random.fold_in(splits[7], 71), 0)
    upper_rows = draw_upper_rows(jax.random.fold_in(splits[7], 71), 0)
    near_list = draw_near_list(jax.random.fold_in(splits[7], 71), 0)
    far_local = draw_far_local(jax.random.fold_in(splits[7], 71), 0)
    far_upper = draw_far_upper(jax.random.fold_in(splits[7], 71), 0)
    return {"points": points, "labels": labels, "skeleton_rows": skeleton_rows, "upper_rows": upper_rows, "near_list": near_list, "far_local": far_local, "far_upper": far_upper}


kernel_scale = 0.04
highest = lax.Precision.HIGHEST


def affinity(left_rows, right_rows):
    cross = jnp.einsum("id,jd->ij", left_rows, right_rows, precision=highest, preferred_element_type=jnp.float32)
    left_sq = jnp.sum(left_rows * left_rows, axis=1)
    right_sq = jnp.sum(right_rows * right_rows, axis=1)
    return jnp.exp((2.0 * cross - left_sq[:, None] - right_sq[None, :]) / kernel_scale)


def product(left_rows, right_rows):
    return jnp.dot(left_rows, right_rows, precision=highest, preferred_element_type=jnp.float32)


def compress(skeleton, members, member_labels, member_mass):
    affine = affinity(skeleton, members)
    totals = jnp.sum(affine, axis=0)
    shares = affine / totals[None, :]
    return product(shares, member_labels), product(shares, member_mass)


def kernel_terms(targets, sources, source_weights, source_mass):
    affine = affinity(targets, sources)
    return product(affine, source_weights), product(affine, source_mass)


def reference(points, labels, skeleton_rows, upper_rows, near_list, far_local, far_upper):
    node_rows = LEAF_DEV * LEAF
    node_points = points.reshape(NODES, node_rows, D)
    node_labels = labels.reshape(NODES, node_rows, C)

    def lower(node_items):
        members, member_labels, rows_taken = node_items
        skeleton = jnp.take(members, rows_taken, axis=0)
        weights, masses = compress(skeleton, members, member_labels, jnp.ones((node_rows,), jnp.float32))
        return skeleton, weights, masses

    lower_points, lower_weights, lower_mass = lax.map(lower, (node_points, node_labels, skeleton_rows))

    def upper(group_items):
        members, member_weights, member_mass, rows_taken = group_items
        skeleton = jnp.take(members, rows_taken, axis=0)
        weights, masses = compress(skeleton, members, member_weights, member_mass)
        return skeleton, weights, masses

    upper_points, upper_weights, upper_mass = lax.map(upper, (
        lower_points.reshape(GROUPS, SUBNODES * SKEL, D),
        lower_weights.reshape(GROUPS, SUBNODES * SKEL, C),
        lower_mass.reshape(GROUPS, SUBNODES * SKEL),
        upper_rows))

    leaf_points = points.reshape(LEAVES, LEAF, D)
    leaf_labels = labels.reshape(LEAVES, LEAF, C)
    diagonal = jnp.eye(LEAF, dtype=jnp.float32)

    def near_one(leaf_items):
        leaf_index, listed = leaf_items
        targets = leaf_points[leaf_index]

        def visit(running, source):
            weight = affinity(targets, leaf_points[source])
            same = (source == leaf_index).astype(jnp.float32)
            weight = weight * (1.0 - same * diagonal)
            return (running[0] + product(weight, leaf_labels[source]), running[1] + jnp.sum(weight, axis=1)), None

        start_pair = (jnp.zeros((LEAF, C), jnp.float32), jnp.zeros((LEAF,), jnp.float32))
        result, _ = lax.scan(visit, start_pair, listed)
        return result

    near_sum, near_count = lax.map(near_one, (jnp.arange(LEAVES, dtype=jnp.int32), near_list))

    def far_one(node_items):
        node_index, local_list, upper_list = node_items
        targets = node_points[node_index]
        outer_group = node_index // SUBNODES
        zero_pair = (jnp.zeros((node_rows, C), jnp.float32), jnp.zeros((node_rows,), jnp.float32))

        def add_local(position, running):
            source = outer_group * SUBNODES + local_list[position]
            add_sum, add_count = kernel_terms(targets, lower_points[source], lower_weights[source], lower_mass[source])
            return running[0] + add_sum, running[1] + add_count

        def add_upper(position, running):
            source = upper_list[position]
            add_sum, add_count = kernel_terms(targets, upper_points[source], upper_weights[source], upper_mass[source])
            return running[0] + add_sum, running[1] + add_count

        local_total = jnp.sum((local_list >= 0).astype(jnp.int32))
        upper_total = jnp.sum((upper_list >= 0).astype(jnp.int32))
        running = lax.fori_loop(0, local_total, add_local, zero_pair)
        return lax.fori_loop(0, upper_total, add_upper, running)

    far_sum, far_count = lax.map(far_one, (jnp.arange(NODES, dtype=jnp.int32), far_local, far_upper))
    numerator = near_sum.reshape(POINTS, C) + far_sum.reshape(POINTS, C)
    denominator = near_count.reshape(POINTS) + far_count.reshape(POINTS)
    return numerator / denominator[:, None]
```

```python
import functools
import math

import jax
import jax.numpy as jnp
from jax import lax
from jax.experimental import pallas as pl
from jax.experimental.pallas import tpu as pltpu
from jax.sharding import PartitionSpec as P

MESH = pl.DeviceIdType.MESH
F32, BF16 = jnp.float32, jnp.bfloat16
ROWS, WIDTH, LABELS, SKEL, LEAF = 512, 768, 64, 256, 256
MSG = 72
CHUNKS = 8
CHUNK = ROWS // CHUNKS
BETA = 25.0 * math.log2(math.e)


def dot_nt(a, b):
    return lax.dot_general(a, b, (((1,), (1,)), ((), ())), preferred_element_type=F32)


def dot_nn(a, b):
    return jnp.dot(a, b, preferred_element_type=F32)


def split(value):
    high = value.astype(BF16)
    return high, (value - high.astype(F32)).astype(BF16)


def kernel(x_ref, lab_ref, skel_ref, urow_ref, near_ref, flocal_ref, fupper_ref, out_ref,
           pts, hi, lo, ncol, nrow, rt, masks, kown, scol, srow,
           contr, contr_in, part, land1, mid, land2, uq, uhi, ulo, uncol,
           up, uphi, uplo, upnrow,
           wp, wp_in, wpart, wland1, wmid, wland2, upw,
           acc, ret_out, ret_in,
           own_sem, s_sem, r_sem):
    gx, gy = lax.axis_index("gx"), lax.axis_index("gy")
    c, j = lax.div(gy, 2), lax.rem(gy, 2)
    y, z = lax.div(gx, 4), lax.rem(gx, 4)
    half = lax.div(c, 2)
    other = 1 - j
    crossed = lax.rem(j + half, 2)
    before, after = lax.rem(c + 3, 4), lax.rem(c + 1, 4)

    def chip(step, core):
        return (gx, lax.rem(c + step, 4) * 2 + core)

    sib = (gx, c * 2 + other)

    def y_peer(step):
        return (lax.rem(y + step, 4) * 4 + z, gy)

    def z_peer(step):
        return (y * 4 + lax.rem(z + step, 4), gy)

    partners = [sib] + [chip(s, k) for s in (1, 3) for k in (j, other)]
    partners += [y_peer(s) for s in (1, 2, 3)] + [z_peer(s) for s in (1, 2, 3)]
    barrier = pltpu.get_barrier_semaphore()
    for partner in partners:
        pl.semaphore_signal(barrier, inc=1, device_id=partner, device_id_type=MESH)
    pl.semaphore_wait(barrier, len(partners))

    started = []

    def send(src, dst, device):
        at = len(started)
        copy = pltpu.make_async_remote_copy(
            src_ref=src, dst_ref=dst, send_sem=s_sem.at[at], recv_sem=r_sem.at[at],
            device_id=device, device_id_type=MESH)
        copy.start()
        started.append(copy)
        return copy

    nodes = [gy, c * 2 + other, before * 2 + j, before * 2 + other, after * 2 + j, after * 2 + other]
    cross_slot, cross_node = 4 + half, after * 2 + crossed

    bulk = {}

    def send_bulk(at):
        rows = pl.ds(at * CHUNK, CHUNK)
        bulk[1, at] = send(x_ref.at[rows], pts.at[2, rows], chip(1, j))
        bulk[3, at] = send(x_ref.at[rows], pts.at[4, rows], chip(3, j))

    own_copy = pltpu.make_async_copy(x_ref, pts.at[0], own_sem)
    own_copy.start()
    send_bulk(0)
    sib_points = send(x_ref, pts.at[1], sib)

    def prep(slot, leaf):
        def body(i, carry):
            rows = pl.ds(pl.multiple_of(leaf * 256 + i * 128, 128), 128)
            value = pts[slot, rows, :]
            high, low = split(value)
            hi[slot, rows, :] = high
            lo[slot, rows, :] = low
            norm = jnp.sum(value * value, axis=1, keepdims=True) * BETA
            wide = jnp.broadcast_to(norm, (128, 128))
            ncol[slot, rows, :] = wide
            nrow[slot, :, rows] = jnp.transpose(wide)[0:8, :]
            return carry
        lax.fori_loop(0, 2, body, 0)

    def affine(t_hi, t_lo, t_col, s_hi, s_lo, s_row):
        cross = dot_nt(t_hi, s_hi) + dot_nt(t_hi, s_lo) + dot_nt(t_lo, s_hi)
        return jnp.exp2(cross * (2.0 * BETA) - jnp.concatenate([t_col, t_col], axis=1) - s_row)

    def product_nt(k, rhs):
        k_hi, k_lo = split(k)
        r_hi, r_lo = split(rhs)
        both = dot_nt(k_hi, jnp.concatenate([r_hi, r_lo], axis=0))
        return both[:, :128] + both[:, 128:] + dot_nt(k_lo, r_hi)

    def product_nn(k, rhs):
        k_hi, k_lo = split(k)
        r_hi, r_lo = split(rhs)
        both = dot_nn(k_hi, jnp.concatenate([r_hi, r_lo], axis=1))
        return both[:, :128] + both[:, 128:] + dot_nn(k_lo, r_hi)

    def leaf_rows(leaf):
        return pl.ds(pl.multiple_of(leaf * 256, 256), 256)

    def block_affine(tb, t, sb, s):
        tr, sr = leaf_rows(t), leaf_rows(s)
        return affine(hi[tb, tr, :], lo[tb, tr, :], ncol[tb, tr, :],
                      hi[sb, sr, :], lo[sb, sr, :], nrow[sb, 0:1, sr])

    lane = lax.broadcasted_iota(jnp.int32, (1, 128), 1)

    def pick(tb, row, at):
        return jnp.sum(jnp.where(lane == at, masks[tb, pl.ds(row, 1), :], 0.0), axis=1, keepdims=True)

    def add_terms(k, tb, t, sb, s, node, target):
        sr = leaf_rows(s)
        rhs = pick(tb, t, 2 * node + s) * rt[sb, 0, :, sr] + pick(tb, 2, node) * rt[sb, 1, :, sr]
        tr = leaf_rows(t)
        acc[target, tr, :] += product_nt(k, rhs)

    def near(tb, sb, s, node, target):
        def body(t, carry):
            add_terms(block_affine(tb, t, sb, s), tb, t, sb, s, node, target)
            return carry
        lax.fori_loop(0, 2, body, 0)

    def far(tb, target, first, count):
        def body(i, carry):
            f = first + lax.div(i, 2)
            t = lax.rem(i, 2)
            q, yy = lax.div(f, 4), lax.rem(f, 4)
            tr = leaf_rows(t)
            fr = leaf_rows(f)
            k = affine(hi[tb, tr, :], lo[tb, tr, :], ncol[tb, tr, :],
                       uphi[fr, :], uplo[fr, :], upnrow[f, 0:1, :])
            weights = upw[q, yy]
            rhs = jnp.concatenate(
                [weights[zz].reshape(64, 128) * pick(tb, 3, yy * 4 + zz) for zz in range(4)], axis=0)
            acc[target, tr, :] += product_nn(k, rhs)
            return carry
        lax.fori_loop(0, 2 * count, body, 0)

    acc[...] = jnp.zeros_like(acc)

    wide_lane = lax.broadcasted_iota(jnp.int32, (ROWS, 64), 1)
    ones_col = jnp.where(wide_lane == 0, 1.0, 0.0)
    rt[0, 0] = jnp.transpose(jnp.concatenate([lab_ref[...], ones_col], axis=1))
    for slot in range(1, 6):
        rt[slot, 0, 64:128, :] = jnp.where(
            lax.broadcasted_iota(jnp.int32, (64, ROWS), 0) == 0, 1.0, 0.0)
        rt[slot, 1, 72:128, :] = jnp.zeros((56, ROWS), F32)

    first_leaf = gx * 16
    for t in range(2):
        row = jnp.zeros((1, 128), F32)
        for e in range(8):
            row += jnp.where(lane == near_ref[t, e] - first_leaf, 1.0, 0.0)
        masks[0, t:t + 1, :] = row
    row = jnp.zeros((1, 128), F32)
    for e in range(7):
        row += jnp.where(lane == flocal_ref[0, e], 1.0, 0.0)
    masks[0, 2:3, :] = row
    row = jnp.zeros((1, 128), F32)
    for e in range(15):
        row += jnp.where(lane == fupper_ref[0, e], 1.0, 0.0)
    masks[0, 3:4, :] = row
    masks[0, 4:8, :] = jnp.zeros((4, 128), F32)

    label_msgs = [send(rt.at[0, 0, 0:64], rt.at[slot, 0, 0:64], device)
                  for slot, device in ((1, sib), (2, chip(1, j)), (4, chip(3, j)))]
    mask_msgs = [send(masks.at[0], masks.at[slot], device)
                 for slot, device in ((1, sib), (2, chip(1, j)), (4, chip(3, j)))]

    skel_t = jnp.where(lax.broadcasted_iota(jnp.int32, (ROWS, SKEL), 0) == skel_ref[...], 1.0, 0.0)
    scol[...] = jnp.broadcast_to(jnp.max(skel_t, axis=1, keepdims=True), (ROWS, 128))
    skel = jnp.transpose(skel_t)
    srow[...] = jnp.broadcast_to(jnp.sum(skel, axis=0, keepdims=True), (8, ROWS))
    chosen_t = jnp.where(
        lax.broadcasted_iota(jnp.int32, (SKEL, SKEL), 0) + gy * SKEL == urow_ref[...], 1.0, 0.0)
    chosen = jnp.transpose(chosen_t).astype(BF16)
    select = dot_nn(chosen, skel.astype(BF16)).astype(BF16)

    own_copy.wait()
    for leaf in range(2):
        prep(0, leaf)

    rows_mine = dot_nn(select, hi[0]) + dot_nn(select, lo[0])
    for q in range(4):
        for h in range(2):
            contr[q, h] = rows_mine[64 * q + 32 * h:64 * q + 32 * h + 32, :]
    contr_msg = send(contr.at[:, other], contr_in, sib)

    def own_tile(i, carry):
        t, s = lax.div(i, 2), lax.rem(i, 2)
        kown[leaf_rows(t), leaf_rows(s)] = block_affine(0, t, 0, s)
        return carry
    lax.fori_loop(0, 4, own_tile, 0)
    inverse = 1.0 / jnp.sum(kown[...] * scol[:, 0:1], axis=0, keepdims=True)
    for t in range(2):
        tr = slice(t * 256, t * 256 + 256)
        total = jnp.zeros((256, 128), F32)
        for s in range(2):
            sr = slice(s * 256, s * 256 + 256)
            total += product_nt(kown[tr, sr] * inverse[:, sr], rt[0, 0, :, sr])
        rt[0, 1, :, tr] = jnp.transpose(total * scol[tr, :])
    weight_msgs = [send(rt.at[0, 1, 0:MSG], rt.at[slot, 1, 0:MSG], device)
                   for slot, device in ((1, sib), (2, chip(1, j)), (4, chip(3, j)))]

    def chip_sum(mine, incoming, total):
        for q in range(4):
            total[q] = mine[q, j] + incoming[q]

    def round_one(total, land):
        return [send(total.at[lax.rem(c + 3, 4)], land.at[0], chip(3, j)),
                send(total.at[lax.rem(c + 2, 4)], land.at[1], chip(1, j))]

    def round_two(total, land, middle, land_two):
        middle[0] = total[c] + land[0]
        middle[1] = total[after] + land[1]
        return [send(middle.at[0], land_two.at[1], chip(3, j)),
                send(middle.at[1], land_two.at[0], chip(1, j))]

    def finish(copies):
        for copy in copies:
            copy.wait_recv()

    contr_msg.wait_recv()
    chip_sum(contr, contr_in, part)
    ones = round_one(part, land1)
    send_bulk(1)

    def own_near(i, carry):
        t, s = lax.div(i, 2), lax.rem(i, 2)
        k = kown[leaf_rows(t), leaf_rows(s)]
        rows = lax.broadcasted_iota(jnp.int32, (256, 256), 0) + t * 256
        cols = lax.broadcasted_iota(jnp.int32, (256, 256), 1) + s * 256
        add_terms(jnp.where(rows == cols, 0.0, k), 0, t, 0, s, gy, 0)
        return carry
    lax.fori_loop(0, 4, own_near, 0)

    finish(ones)
    twos = round_two(part, land1, mid, land2)
    send_bulk(2)
    sib_points.wait_recv()
    label_msgs[0].wait_recv()
    mask_msgs[0].wait_recv()
    weight_msgs[0].wait_recv()
    for leaf in range(2):
        prep(1, leaf)

    finish(twos)
    quarter0 = mid[0] + land2[0]
    quarter1 = mid[1] + land2[1]
    uq[c, j] = quarter0
    uq[after, j] = quarter1
    up[0, y, z, j] = quarter0
    up[1, y, z, j] = quarter1
    threes = [send(uq.at[after, j], uq.at[after, j], chip(3, j)),
              send(uq.at[c, j], uq.at[c, j], chip(1, j))]

    def phase_one(buffer):
        return ([send(buffer.at[0, y, z, j], buffer.at[0, y, z, j], y_peer(s)) for s in (1, 2, 3)]
                + [send(buffer.at[1, y, z, j], buffer.at[1, y, z, j], z_peer(s)) for s in (1, 2, 3)])

    def phase_two(buffer):
        return ([send(buffer.at[0, :, z, j], buffer.at[0, :, z, j], z_peer(s)) for s in (1, 2, 3)]
                + [send(buffer.at[1, y, :, j], buffer.at[1, y, :, j], y_peer(s)) for s in (1, 2, 3)])

    up_one = phase_one(up)
    send_bulk(3)

    near(0, 1, 0, nodes[1], 0)
    near(0, 1, 1, nodes[1], 0)

    finish(threes)
    share = send(uq.at[:, j], uq.at[:, j], sib)
    send_bulk(4)
    finish(up_one)
    up_two = phase_two(up)
    share.wait_recv()

    def prep_upper(i, carry):
        value = uq[i].reshape(64, WIDTH)
        rows = pl.ds(pl.multiple_of(i * 64, 64), 64)
        high, low = split(value)
        uhi[rows, :] = high
        ulo[rows, :] = low
        norm = jnp.sum(value * value, axis=1, keepdims=True) * BETA
        uncol[rows, :] = jnp.broadcast_to(norm, (64, 128))
        return carry
    lax.fori_loop(0, 4, prep_upper, 0)
    partial_sum = jnp.zeros((SKEL, 128), F32)
    for s in range(2):
        sr = slice(s * 256, s * 256 + 256)
        k = affine(uhi[...], ulo[...], uncol[...], hi[0, sr, :], lo[0, sr, :], nrow[0, 0:1, sr])
        total = jnp.sum(k, axis=0, keepdims=True)
        taken = srow[0:1, sr] > 0.0
        shares = k * jnp.where(taken, 1.0 / total, 0.0)
        partial_sum += product_nt(shares, rt[0, 1, :, sr])
    for q in range(4):
        for h in range(2):
            wp[q, h] = partial_sum[64 * q + 32 * h:64 * q + 32 * h + 32, :]
    wp_msg = send(wp.at[:, other], wp_in, sib)
    send_bulk(5)

    for copy in label_msgs[1:] + mask_msgs[1:] + weight_msgs[1:]:
        copy.wait_recv()
    forward = []
    for slot in (2, 4):
        forward += [send(rt.at[slot, :, 0:MSG], rt.at[slot + 1, :, 0:MSG], sib),
                    send(masks.at[slot], masks.at[slot + 1], sib)]
    wp_msg.wait_recv()
    chip_sum(wp, wp_in, wpart)
    w_ones = round_one(wpart, wland1)
    send_bulk(6)

    def leaf_arrives(leaf):
        copies = []
        for step, slot in ((1, 2), (3, 4)):
            for at in range(leaf * CHUNKS // 2, (leaf + 1) * CHUNKS // 2):
                bulk[step, at].wait_recv()
            rows = slice(leaf * 256, leaf * 256 + 256)
            copies.append(send(pts.at[slot, rows], pts.at[slot + 1, rows], sib))
        return copies

    def prep_up(f, carry):
        q, yy = lax.div(f, 4), lax.rem(f, 4)
        for zz in range(4):
            value = up[q, yy, zz].reshape(64, WIDTH)
            rows = pl.ds(pl.multiple_of(f * 256 + zz * 64, 64), 64)
            high, low = split(value)
            uphi[rows, :] = high
            uplo[rows, :] = low
            norm = jnp.sum(value * value, axis=1, keepdims=True) * BETA
            uncol[zz * 64:zz * 64 + 64, :] = jnp.broadcast_to(norm, (64, 128))
        upnrow[f] = jnp.transpose(uncol[...])[0:8, :]
        return carry

    finish(w_ones)
    w_twos = round_two(wpart, wland1, wmid, wland2)
    send_bulk(7)
    first = leaf_arrives(0)
    for slot in (2, 4):
        prep(slot, 0)
        near(0, slot, 0, nodes[slot], 0)

    finish(w_twos)
    upw[0, y, z, j] = wmid[0] + wland2[0]
    upw[1, y, z, j] = wmid[1] + wland2[1]
    w_up_one = phase_one(upw)

    finish(up_two)
    up_share = send(up.at[:, :, :, j], up.at[:, :, :, j], sib)
    finish(forward)
    finish(first)
    for slot in (3, 5):
        prep(slot, 0)
        near(0, slot, 0, nodes[slot], 0)
    finish(w_up_one)
    w_up_two = phase_two(upw)
    up_share.wait_recv()
    lax.fori_loop(0, 8, prep_up, 0)
    finish(w_up_two)
    w_share = send(upw.at[:, :, :, j], upw.at[:, :, :, j], sib)
    w_share.wait_recv()
    far(0, 0, 0, 8)

    second = leaf_arrives(1)
    for slot in (2, 4):
        prep(slot, 1)
    finish(second)
    for slot in (3, 5):
        prep(slot, 1)

    for s in range(2):
        near(2, cross_slot, s, cross_node, 1)
    far(2, 1, 4, 4)
    ret_out[0] = jnp.transpose(acc[1])
    back_before = send(ret_out.at[0, 0:MSG], ret_in.at[0, 0:MSG], chip(3, j))
    for s in range(2):
        near(cross_slot, 2, s, nodes[2], 2)
    far(cross_slot, 2, 0, 4)
    ret_out[1] = jnp.transpose(acc[2])
    back_after = send(ret_out.at[1, 0:MSG], ret_in.at[1, 0:MSG], chip(1, crossed))

    for slot in (2, 4, 3, 5):
        near(0, slot, 1, nodes[slot], 0)
    back_before.wait_recv()
    back_after.wait_recv()
    returned = jnp.transpose(ret_in[0] + ret_in[1])
    out_ref[...] = acc[0] + returned

    for copy in started:
        copy.wait_send()


N_COPIES = 96


def on_device(points, labels, skeleton_rows, upper_rows, near_list, far_local, far_upper):
    vmem = pl.BlockSpec(memory_space=pltpu.VMEM)
    smem = pl.BlockSpec(memory_space=pltpu.SMEM)
    sums = pl.pallas_call(
        kernel,
        out_shape=jax.ShapeDtypeStruct((ROWS, 128), F32),
        in_specs=[pl.BlockSpec(memory_space=pl.ANY), vmem, vmem, vmem, smem, smem, smem],
        out_specs=vmem,
        scratch_shapes=[
            pltpu.VMEM((6, ROWS, WIDTH), F32),
            pltpu.VMEM((6, ROWS, WIDTH), BF16),
            pltpu.VMEM((6, ROWS, WIDTH), BF16),
            pltpu.VMEM((6, ROWS, 128), F32),
            pltpu.VMEM((6, 8, ROWS), F32),
            pltpu.VMEM((6, 2, 128, ROWS), F32),
            pltpu.VMEM((6, 8, 128), F32),
            pltpu.VMEM((ROWS, ROWS), F32),
            pltpu.VMEM((ROWS, 128), F32),
            pltpu.VMEM((8, ROWS), F32),
            pltpu.VMEM((4, 2, 32, WIDTH), F32),
            pltpu.VMEM((4, 32, WIDTH), F32),
            pltpu.VMEM((4, 32, WIDTH), F32),
            pltpu.VMEM((2, 32, WIDTH), F32),
            pltpu.VMEM((2, 32, WIDTH), F32),
            pltpu.VMEM((2, 32, WIDTH), F32),
            pltpu.VMEM((4, 2, 32, WIDTH), F32),
            pltpu.VMEM((SKEL, WIDTH), BF16),
            pltpu.VMEM((SKEL, WIDTH), BF16),
            pltpu.VMEM((SKEL, 128), F32),
            pltpu.VMEM((2, 4, 4, 2, 32, WIDTH), F32),
            pltpu.VMEM((2048, WIDTH), BF16),
            pltpu.VMEM((2048, WIDTH), BF16),
            pltpu.VMEM((8, 8, 256), F32),
            pltpu.VMEM((4, 2, 32, 128), F32),
            pltpu.VMEM((4, 32, 128), F32),
            pltpu.VMEM((4, 32, 128), F32),
            pltpu.VMEM((2, 32, 128), F32),
            pltpu.VMEM((2, 32, 128), F32),
            pltpu.VMEM((2, 32, 128), F32),
            pltpu.VMEM((2, 4, 4, 2, 32, 128), F32),
            pltpu.VMEM((3, ROWS, 128), F32),
            pltpu.VMEM((2, 128, ROWS), F32),
            pltpu.VMEM((2, 128, ROWS), F32),
            pltpu.SemaphoreType.DMA,
            pltpu.SemaphoreType.DMA((N_COPIES,)),
            pltpu.SemaphoreType.DMA((N_COPIES,)),
        ],
        compiler_params=pltpu.CompilerParams(
            collective_id=0, has_side_effects=True, vmem_limit_bytes=62 * 1024 * 1024),
        cost_estimate=pl.CostEstimate(
            flops=64 * 6 * 256 * 256 * 768, bytes_accessed=2 * 1024 * 1024, transcendentals=64 * 256 * 256),
    )(points, labels, skeleton_rows, upper_rows, near_list, far_local, far_upper)
    return sums[:, :LABELS] / sums[:, LABELS:LABELS + 1]


def solution(mesh):
    return jax.shard_map(
        on_device,
        mesh=mesh,
        in_specs=(
            P(("gx", "gy"), None),
            P(("gx", "gy"), None),
            P(("gx", "gy"), None),
            P("gx", None),
            P(("gx", "gy"), None),
            P(("gx", "gy"), None),
            P(("gx", "gy"), None),
        ),
        out_specs=P(("gx", "gy"), None),
        check_vma=False,
    )
```

```python
import functools
import math

import jax
import jax.numpy as jnp
from jax import lax
from jax.experimental import pallas as pl
from jax.experimental.pallas import tpu as pltpu
from jax.sharding import PartitionSpec as P

MESH = pl.DeviceIdType.MESH
F32, BF16 = jnp.float32, jnp.bfloat16
ROWS, WIDTH, LABELS, SKEL, LEAF = 512, 768, 64, 256, 256
MSG = 72
CHUNKS = (32, 32, 32, 32, 64, 64, 128, 128)
BETA = 25.0 * math.log2(math.e)


def dot_nt(a, b):
    return lax.dot_general(a, b, (((1,), (1,)), ((), ())), preferred_element_type=F32)


def dot_nn(a, b):
    return jnp.dot(a, b, preferred_element_type=F32)


def split(value):
    high = value.astype(BF16)
    return high, (value - high.astype(F32)).astype(BF16)


def kernel(x_ref, lab_ref, skel_ref, urow_ref, near_ref, flocal_ref, fupper_ref, out_ref,
           pts, hi, lo, ncol, nrow, rt, masks, kown, scol, srow,
           contr, contr_in, part, land1, mid, land2, uq, uhi, ulo, uncol,
           up, uphi, uplo, upnrow,
           wp, wp_in, wpart, wland1, wmid, wland2, upw, kf_hi, kf_lo, kn_hi, kn_lo,
           acc, ret_out, ret_in,
           own_sem, s_sem, r_sem):
    gx, gy = lax.axis_index("gx"), lax.axis_index("gy")
    c, j = lax.div(gy, 2), lax.rem(gy, 2)
    y, z = lax.div(gx, 4), lax.rem(gx, 4)
    half = lax.div(c, 2)
    other = 1 - j
    crossed = lax.rem(j + half, 2)
    before, after = lax.rem(c + 3, 4), lax.rem(c + 1, 4)

    def chip(step, core):
        return (gx, lax.rem(c + step, 4) * 2 + core)

    sib = (gx, c * 2 + other)

    def y_peer(step):
        return (lax.rem(y + step, 4) * 4 + z, gy)

    def z_peer(step):
        return (y * 4 + lax.rem(z + step, 4), gy)

    own_copies = [pltpu.make_async_copy(x_ref.at[pl.ds(256 * leaf, 256)], pts.at[leaf], own_sem.at[leaf])
                  for leaf in range(2)]
    own_copies.append(pltpu.make_async_copy(lab_ref, rt.at[0, 0, 0:64], own_sem.at[2]))
    for copy in own_copies:
        copy.start()

    partners = [sib] + [chip(s, k) for s in (1, 3) for k in (j, other)]
    partners += [y_peer(s) for s in (1, 2, 3)] + [z_peer(s) for s in (1, 2, 3)]
    barrier = pltpu.get_barrier_semaphore()
    for partner in partners:
        pl.semaphore_signal(barrier, inc=1, device_id=partner, device_id_type=MESH)
    pl.semaphore_wait(barrier, len(partners))

    started = []

    def send(src, dst, device):
        at = len(started)
        copy = pltpu.make_async_remote_copy(
            src_ref=src, dst_ref=dst, send_sem=s_sem.at[at], recv_sem=r_sem.at[at],
            device_id=device, device_id_type=MESH)
        copy.start()
        started.append(copy)
        return copy

    def finish(copies):
        for copy in copies:
            copy.wait_recv()

    nodes = [gy, c * 2 + other, before * 2 + j, before * 2 + other, after * 2 + j, after * 2 + other]
    cross_slot, cross_node, cross_leaf = 4 + half, after * 2 + crossed, 5 + 4 * half

    bulk = {1: [], 3: []}

    def send_bulk(count=1):
        for _ in range(count):
            at = len(bulk[1])
            first, size = sum(CHUNKS[:at]), CHUNKS[at]
            leaf, rows = first // 256, pl.ds(first % 256, size)
            src = x_ref.at[pl.ds(first, size)]
            bulk[1].append(send(src, pts.at[4 + 2 * leaf, rows], chip(1, j)))
            bulk[3].append(send(src, pts.at[5 + 2 * leaf, rows], chip(3, j)))

    label_msgs = [send(lab_ref, rt.at[slot, 0, 0:64], device)
                  for slot, device in ((2, chip(1, j)), (4, chip(3, j)), (1, sib))]
    send_bulk()
    sib_points = [send(x_ref.at[pl.ds(256 * leaf, 256)], pts.at[2 + leaf], sib) for leaf in range(2)]

    skel_t = jnp.where(lax.broadcasted_iota(jnp.int32, (ROWS, SKEL), 0) == skel_ref[...], 1.0, 0.0)
    scol[...] = jnp.broadcast_to(jnp.max(skel_t, axis=1, keepdims=True), (ROWS, 128))
    skel = jnp.transpose(skel_t)
    srow[...] = jnp.broadcast_to(jnp.sum(skel, axis=0, keepdims=True), (8, ROWS))
    chosen_t = jnp.where(
        lax.broadcasted_iota(jnp.int32, (SKEL, SKEL), 0) + gy * SKEL == urow_ref[...], 1.0, 0.0)
    chosen = jnp.transpose(chosen_t).astype(BF16)
    select = dot_nn(chosen, skel.astype(BF16)).astype(BF16)

    def prep(leaf, first, size):
        def body(i, carry):
            rows = pl.ds(pl.multiple_of(first + i * 128, 128), 128)
            value = pts[leaf, rows, :]
            high, low = split(value)
            hi[leaf, rows, :] = high
            lo[leaf, rows, :] = low
            norm = jnp.sum(value * value, axis=1, keepdims=True) * BETA
            wide = jnp.broadcast_to(norm, (128, 128))
            ncol[leaf, rows, :] = wide
            nrow[leaf, :, rows] = jnp.transpose(wide)[0:8, :]
            return carry
        lax.fori_loop(0, size // 128, body, 0)

    def many(parts, axis):
        return parts[0] if len(parts) == 1 else jnp.concatenate(parts, axis=axis)

    def affine(targets, sources):
        t_hi, t_lo, t_col = targets
        s_hi, s_lo, s_row = sources
        cross = dot_nt(t_hi, s_hi) + dot_nt(t_hi, s_lo) + dot_nt(t_lo, s_hi)
        wide = jnp.concatenate([t_col] * (s_hi.shape[0] // 128), axis=1)
        return jnp.exp2(cross * (2.0 * BETA) - wide - s_row)

    def as_targets(pieces):
        return (many([hi[l, f:f + n, :] for l, f, n in pieces], 0),
                many([lo[l, f:f + n, :] for l, f, n in pieces], 0),
                many([ncol[l, f:f + n, :] for l, f, n in pieces], 0))

    def as_sources(pieces):
        return (many([hi[l, f:f + n, :] for l, f, n in pieces], 0),
                many([lo[l, f:f + n, :] for l, f, n in pieces], 0),
                many([nrow[l, 0:1, f:f + n] for l, f, n in pieces], 1))

    def product_nt(k, rhs):
        k_hi, k_lo = split(k)
        r_hi, r_lo = split(rhs)
        both = dot_nt(k_hi, jnp.concatenate([r_hi, r_lo], axis=0))
        return both[:, :128] + both[:, 128:] + dot_nt(k_lo, r_hi)

    def product_nn(k_hi, k_lo, rhs):
        r_hi, r_lo = split(rhs)
        both = dot_nn(k_hi, jnp.concatenate([r_hi, r_lo], axis=1))
        return both[:, :128] + both[:, 128:] + dot_nn(k_lo, r_hi)

    lane = lax.broadcasted_iota(jnp.int32, (1, 128), 1)

    def pick(slot, row, at):
        return jnp.sum(jnp.where(lane == at, masks[slot, row:row + 1, :], 0.0), axis=1, keepdims=True)

    def near_rhs(slot, t, sources):
        return many([pick(slot, t, 2 * node + s) * rt[sl, 0, :, 256 * s + f:256 * s + f + n]
                     + pick(slot, 2, node) * rt[sl, 1, :, 256 * s + f:256 * s + f + n]
                     for sl, node, s, f, n in sources], 1)

    def near(target, slot, targets, source_pieces, source_terms):
        k = affine(as_targets([(l, f, n) for l, _, f, n in targets]), as_sources(source_pieces))
        at = 0
        for _, t, f, n in targets:
            acc[target, 256 * t + f:256 * t + f + n, :] += product_nt(
                k[at:at + n], near_rhs(slot, t, source_terms))
            at += n

    OWN = [(0, 0, 0, 256), (1, 1, 0, 256)]

    def up_sources(q, m):
        rows = pl.ds(pl.multiple_of((q * 4 + m) * 256, 256), 256)
        return uphi[rows, :], uplo[rows, :], upnrow[q * 4 + m, 0:1, :]

    def up_pair(parts):
        loaded = [up_sources(q, m) for q, m in parts]
        return (many([p[0] for p in loaded], 0), many([p[1] for p in loaded], 0), many([p[2] for p in loaded], 1))

    def up_rhs(slot, q, m):
        weights = upw[q, m]
        parts = []
        for n in range(4):
            cluster = n * 4 + m if q == 0 else m * 4 + n
            parts.append(weights[n].reshape(64, 128) * pick(slot, 3, cluster))
        return jnp.concatenate(parts, axis=0)

    acc[...] = jnp.zeros_like(acc)

    for slot in range(6):
        rt[slot, 0, 64:128, :] = jnp.where(
            lax.broadcasted_iota(jnp.int32, (64, ROWS), 0) == 0, 1.0, 0.0)
        rt[slot, 1, 72:128, :] = jnp.zeros((56, ROWS), F32)

    own_copies[0].wait()
    own_copies[1].wait()
    for leaf in range(2):
        prep(leaf, 0, 256)

    rows_mine = jnp.zeros((SKEL, WIDTH), F32)
    for leaf in range(2):
        chosen_rows = select[:, 256 * leaf:256 * leaf + 256]
        rows_mine += dot_nn(chosen_rows, hi[leaf]) + dot_nn(chosen_rows, lo[leaf])
    for q in range(4):
        for h in range(2):
            contr[q, h] = rows_mine[64 * q + 32 * h:64 * q + 32 * h + 32, :]
    contr_msg = send(contr.at[:, other], contr_in, sib)

    def mask_row(entries):
        row = jnp.zeros((1, 128), F32)
        for entry in entries:
            row += jnp.where(lane == entry, 1.0, 0.0)
        return row

    for t in range(2):
        masks[0, t:t + 1, :] = mask_row([near_ref[t, e] - gx * 16 for e in range(8)])
    masks[0, 2:3, :] = mask_row([flocal_ref[0, e] for e in range(7)])
    masks[0, 3:4, :] = mask_row([fupper_ref[0, e] for e in range(15)])
    masks[0, 4:8, :] = jnp.zeros((4, 128), F32)
    mask_msgs = [send(masks.at[0], masks.at[slot], device)
                 for slot, device in ((1, sib), (2, chip(1, j)), (4, chip(3, j)))]

    def chip_sum(mine, incoming, total):
        for q in range(4):
            total[q] = mine[q, j] + incoming[q]

    def round_one(total, land):
        return [send(total.at[lax.rem(c + 3, 4)], land.at[0], chip(3, j)),
                send(total.at[lax.rem(c + 2, 4)], land.at[1], chip(1, j))]

    def round_two(total, land, middle, land_two):
        middle[0] = total[c] + land[0]
        middle[1] = total[after] + land[1]
        return [send(middle.at[0], land_two.at[1], chip(3, j)),
                send(middle.at[1], land_two.at[0], chip(1, j))]

    contr_msg.wait_recv()
    chip_sum(contr, contr_in, part)
    ones = round_one(part, land1)
    send_bulk()

    kown[...] = affine(as_targets([(0, 0, 256), (1, 0, 256)]), as_sources([(0, 0, 256), (1, 0, 256)]))
    own_copies[2].wait()
    inverse = 1.0 / jnp.sum(kown[...] * scol[:, 0:1], axis=0, keepdims=True)
    lower = product_nt(kown[...] * inverse, rt[0, 0]) * scol[...]

    finish(ones)
    twos = round_two(part, land1, mid, land2)
    send_bulk()

    rt[0, 1] = jnp.transpose(lower)

    rows_at = lax.broadcasted_iota(jnp.int32, (256, ROWS), 0)
    cols_at = lax.broadcasted_iota(jnp.int32, (256, ROWS), 1)
    for t in range(2):
        k = jnp.where(rows_at + 256 * t == cols_at, 0.0, kown[256 * t:256 * t + 256, :])
        acc[0, 256 * t:256 * t + 256, :] += product_nt(
            k, near_rhs(0, t, [(0, gy, 0, 0, 256), (0, gy, 1, 0, 256)]))

    finish(twos)
    quarter0 = mid[0] + land2[0]
    quarter1 = mid[1] + land2[1]
    uq[c, j] = quarter0
    uq[after, j] = quarter1
    up[0, z, y, j] = quarter0
    up[1, y, z, j] = quarter1
    threes = [send(uq.at[after, j], uq.at[after, j], chip(3, j)),
              send(uq.at[c, j], uq.at[c, j], chip(1, j))]

    def phase_one(buffer):
        return ([send(buffer.at[0, z, y, j], buffer.at[0, z, y, j], y_peer(s)) for s in (1, 3, 2)]
                + [send(buffer.at[1, y, z, j], buffer.at[1, y, z, j], z_peer(s)) for s in (1, 3, 2)])

    def phase_two(buffer):
        return {s: [send(buffer.at[0, z, :, j], buffer.at[0, z, :, j], z_peer(s)),
                    send(buffer.at[1, y, :, j], buffer.at[1, y, :, j], y_peer(s))] for s in (1, 3, 2)}

    def majors(step):
        return lax.rem(z + 4 - step, 4), lax.rem(y + 4 - step, 4)

    def share_step(buffer, step):
        m0, m1 = majors(step)
        return [send(buffer.at[0, m0, :, j], buffer.at[0, m0, :, j], sib),
                send(buffer.at[1, m1, :, j], buffer.at[1, m1, :, j], sib)]

    up_one = phase_one(up)
    send_bulk()
    weight_msgs = [send(rt.at[0, 1, 0:MSG], rt.at[slot, 1, 0:MSG], device)
                   for slot, device in ((1, sib), (2, chip(1, j)), (4, chip(3, j)))]

    finish(sib_points)
    label_msgs[2].wait_recv()
    mask_msgs[0].wait_recv()
    for leaf in range(2):
        prep(2 + leaf, 0, 256)

    finish(up_one)
    up_two = phase_two(up)
    up_share = {0: share_step(up, 0)}

    finish(threes)
    share = send(uq.at[:, j], uq.at[:, j], sib)
    weight_msgs[0].wait_recv()
    near(0, 0, OWN, [(2, 0, 256), (3, 0, 256)], [(1, nodes[1], 0, 0, 256), (1, nodes[1], 1, 0, 256)])
    send_bulk()
    share.wait_recv()

    def prep_upper(i, carry):
        value = uq[i].reshape(64, WIDTH)
        rows = pl.ds(pl.multiple_of(i * 64, 64), 64)
        high, low = split(value)
        uhi[rows, :] = high
        ulo[rows, :] = low
        norm = jnp.sum(value * value, axis=1, keepdims=True) * BETA
        uncol[rows, :] = jnp.broadcast_to(norm, (64, 128))
        return carry
    lax.fori_loop(0, 4, prep_upper, 0)
    k = affine((uhi[...], ulo[...], uncol[...]), as_sources([(0, 0, 256), (1, 0, 256)]))
    total = jnp.sum(k, axis=0, keepdims=True)
    shares = k * jnp.where(srow[0:1, :] > 0.0, 1.0 / total, 0.0)
    partial_sum = product_nt(shares, rt[0, 1])
    for q in range(4):
        for h in range(2):
            wp[q, h] = partial_sum[64 * q + 32 * h:64 * q + 32 * h + 32, :]
    wp_msg = send(wp.at[:, other], wp_in, sib)

    def prep_up(q, m):
        def body(n, carry):
            value = up[q, m, n].reshape(64, WIDTH)
            rows = pl.ds(pl.multiple_of((q * 4 + m) * 256 + n * 64, 64), 64)
            high, low = split(value)
            uphi[rows, :] = high
            uplo[rows, :] = low
            norm = jnp.sum(value * value, axis=1, keepdims=True) * BETA
            uncol[pl.ds(pl.multiple_of(n * 64, 64), 64), :] = jnp.broadcast_to(norm, (64, 128))
            return carry
        lax.fori_loop(0, 4, body, 0)
        upnrow[q * 4 + m] = jnp.transpose(uncol[...])[0:8, :]

    def far_own(step):
        m0, m1 = majors(step)
        prep_up(0, m0)
        prep_up(1, m1)
        k_hi, k_lo = split(affine(as_targets([(0, 0, 256), (1, 0, 256)]), up_pair([(0, m0), (1, m1)])))
        kf_hi[step] = k_hi
        kf_lo[step] = k_lo

    finish(up_share[0])
    far_own(0)

    wp_msg.wait_recv()
    chip_sum(wp, wp_in, wpart)
    w_ones = round_one(wpart, wland1)
    send_bulk()

    finish(label_msgs[:2] + mask_msgs[1:] + weight_msgs[1:])
    forward = []
    for slot in (2, 4):
        forward += [send(rt.at[slot, :, 0:MSG], rt.at[slot + 1, :, 0:MSG], sib),
                    send(masks.at[slot], masks.at[slot + 1], sib)]
    finish(w_ones)
    w_twos = round_two(wpart, wland1, wmid, wland2)
    send_bulk(len(CHUNKS) - len(bulk[1]))

    finish(up_two[1])
    up_share[1] = share_step(up, 1)
    finish(up_two[3])
    up_share[3] = share_step(up, 3)

    finish(w_twos)
    upw[0, z, y, j] = wmid[0] + wland2[0]
    upw[1, y, z, j] = wmid[1] + wland2[1]
    w_up_one = phase_one(upw)

    finish(up_share[1])
    far_own(1)
    finish(up_share[3])
    far_own(3)

    taken = [0]

    def piece_arrives(leaf, first, size):
        end = 256 * leaf + first + size
        while taken[0] < len(CHUNKS) and sum(CHUNKS[:taken[0] + 1]) <= end:
            bulk[1][taken[0]].wait_recv()
            bulk[3][taken[0]].wait_recv()
            taken[0] += 1
        rows = pl.ds(first, size)
        return [send(pts.at[4 + 2 * leaf + side, rows], pts.at[8 + 2 * leaf + side, rows], sib)
                for side in range(2)]

    passed = piece_arrives(0, 0, 256)
    for buffer in (4, 5):
        prep(buffer, 0, 256)
    near(0, 0, OWN, [(4, 0, 256), (5, 0, 256)], [(2, nodes[2], 0, 0, 256), (4, nodes[4], 0, 0, 256)])
    finish(passed)
    finish(forward)
    for buffer in (8, 9):
        prep(buffer, 0, 256)
    near(0, 0, OWN, [(8, 0, 256), (9, 0, 256)], [(3, nodes[3], 0, 0, 256), (5, nodes[5], 0, 0, 256)])

    finish(up_two[2])
    up_share[2] = share_step(up, 2)
    finish(w_up_one)
    w_up_two = phase_two(upw)
    finish(up_share[2])
    far_own(2)

    def far_kernel(target_pieces, q, m):
        return split(affine(as_targets(target_pieces), up_pair([(q, m), (q, m + 1)])))

    for side, (leaf, q) in enumerate(((4, 1), (cross_leaf, 0))):
        for m in (0, 2):
            k_hi, k_lo = far_kernel([(leaf, 0, 256)], q, m)
            kn_hi[side, m // 2] = k_hi
            kn_lo[side, m // 2] = k_lo

    for s in (1, 3, 2):
        finish(w_up_two[s])
    w_share = [send(upw.at[:, :, :, j], upw.at[:, :, :, j], sib)]
    finish(w_share)

    for step in range(4):
        m0, m1 = majors(step)
        rhs = jnp.concatenate([up_rhs(0, 0, m0), up_rhs(0, 1, m1)], axis=0)
        acc[0] += product_nn(kf_hi[step], kf_lo[step], rhs)

    def far_terms(slot, q, m):
        return jnp.concatenate([up_rhs(slot, q, m), up_rhs(slot, q, m + 1)], axis=0)

    for side, (slot, q) in enumerate(((2, 1), (cross_slot, 0))):
        for m in (0, 2):
            acc[1 + side, 0:256, :] += product_nn(kn_hi[side, m // 2], kn_lo[side, m // 2], far_terms(slot, q, m))

    for first in (0, 128):
        passed = piece_arrives(1, first, 128)
        for buffer in (6, 7):
            prep(buffer, first, 128)
        finish(passed)
        for buffer in (10, 11):
            prep(buffer, first, 128)

        def own_piece():
            near(0, 0, OWN, [(b, first, 128) for b in (6, 7, 10, 11)],
                 [(sl, nodes[sl], 1, first, 128) for sl in (2, 4, 3, 5)])

        if first == 0:
            own_piece()
        for side, (slot, leaf, q) in enumerate(((2, 6, 1), (cross_slot, cross_leaf + 2, 0))):
            for m in (0, 2):
                k_hi, k_lo = far_kernel([(leaf, first, 128)], q, m)
                acc[1 + side, 256 + first:384 + first, :] += product_nn(k_hi, k_lo, far_terms(slot, q, m))

    sides = ((2, nodes[2], 4), (cross_slot, cross_node, cross_leaf))
    backs = []
    for side in range(2):
        slot, _, leaf = sides[side]
        from_slot, from_node, from_leaf = sides[1 - side]
        near(1 + side, slot, [(leaf, 0, 0, 256), (leaf + 2, 1, 0, 256)],
             [(from_leaf, 0, 256), (from_leaf + 2, 0, 256)],
             [(from_slot, from_node, 0, 0, 256), (from_slot, from_node, 1, 0, 256)])
        ret_out[side] = jnp.transpose(acc[1 + side])
        backs.append(send(ret_out.at[side, 0:MSG], ret_in.at[side, 0:MSG],
                          chip(3, j) if side == 0 else chip(1, crossed)))
    own_piece()
    finish(backs)
    sums = jnp.transpose(acc[0])[0:MSG] + ret_in[0, 0:MSG] + ret_in[1, 0:MSG]
    out_ref[...] = sums[0:LABELS] / sums[LABELS:LABELS + 1]

    for copy in started:
        copy.wait_send()


N_COPIES = 110


def on_device(points, labels, skeleton_rows, upper_rows, near_list, far_local, far_upper):
    vmem = pl.BlockSpec(memory_space=pltpu.VMEM)
    smem = pl.BlockSpec(memory_space=pltpu.SMEM)
    hbm = pl.BlockSpec(memory_space=pl.ANY)
    result = pl.pallas_call(
        kernel,
        out_shape=jax.ShapeDtypeStruct((LABELS, ROWS), F32),
        in_specs=[hbm, hbm, vmem, vmem, smem, smem, smem],
        out_specs=vmem,
        scratch_shapes=[
            pltpu.VMEM((12, LEAF, WIDTH), F32),
            pltpu.VMEM((12, LEAF, WIDTH), BF16),
            pltpu.VMEM((12, LEAF, WIDTH), BF16),
            pltpu.VMEM((12, LEAF, 128), F32),
            pltpu.VMEM((12, 8, LEAF), F32),
            pltpu.VMEM((6, 2, 128, ROWS), F32),
            pltpu.VMEM((6, 8, 128), F32),
            pltpu.VMEM((ROWS, ROWS), F32),
            pltpu.VMEM((ROWS, 128), F32),
            pltpu.VMEM((8, ROWS), F32),
            pltpu.VMEM((4, 2, 32, WIDTH), F32),
            pltpu.VMEM((4, 32, WIDTH), F32),
            pltpu.VMEM((4, 32, WIDTH), F32),
            pltpu.VMEM((2, 32, WIDTH), F32),
            pltpu.VMEM((2, 32, WIDTH), F32),
            pltpu.VMEM((2, 32, WIDTH), F32),
            pltpu.VMEM((4, 2, 32, WIDTH), F32),
            pltpu.VMEM((SKEL, WIDTH), BF16),
            pltpu.VMEM((SKEL, WIDTH), BF16),
            pltpu.VMEM((SKEL, 128), F32),
            pltpu.VMEM((2, 4, 4, 2, 32, WIDTH), F32),
            pltpu.VMEM((2048, WIDTH), BF16),
            pltpu.VMEM((2048, WIDTH), BF16),
            pltpu.VMEM((8, 8, 256), F32),
            pltpu.VMEM((4, 2, 32, 128), F32),
            pltpu.VMEM((4, 32, 128), F32),
            pltpu.VMEM((4, 32, 128), F32),
            pltpu.VMEM((2, 32, 128), F32),
            pltpu.VMEM((2, 32, 128), F32),
            pltpu.VMEM((2, 32, 128), F32),
            pltpu.VMEM((2, 4, 4, 2, 32, 128), F32),
            pltpu.VMEM((4, ROWS, ROWS), BF16),
            pltpu.VMEM((4, ROWS, ROWS), BF16),
            pltpu.VMEM((2, 2, LEAF, ROWS), BF16),
            pltpu.VMEM((2, 2, LEAF, ROWS), BF16),
            pltpu.VMEM((3, ROWS, 128), F32),
            pltpu.VMEM((2, 128, ROWS), F32),
            pltpu.VMEM((2, 128, ROWS), F32),
            pltpu.SemaphoreType.DMA((3,)),
            pltpu.SemaphoreType.DMA((N_COPIES,)),
            pltpu.SemaphoreType.DMA((N_COPIES,)),
        ],
        compiler_params=pltpu.CompilerParams(
            collective_id=0, has_side_effects=True, vmem_limit_bytes=62 * 1024 * 1024),
        cost_estimate=pl.CostEstimate(
            flops=64 * 6 * 256 * 256 * 768, bytes_accessed=2 * 1024 * 1024, transcendentals=64 * 256 * 256),
    )(points, labels.T, skeleton_rows, upper_rows, near_list, far_local, far_upper)
    return result.T


def solution(mesh):
    return jax.shard_map(
        on_device,
        mesh=mesh,
        in_specs=(
            P(("gx", "gy"), None),
            P(("gx", "gy"), None),
            P(("gx", "gy"), None),
            P("gx", None),
            P(("gx", "gy"), None),
            P(("gx", "gy"), None),
            P(("gx", "gy"), None),
        ),
        out_specs=P(("gx", "gy"), None),
        check_vma=False,
    )
```

```python
import functools
import math

import jax
import jax.numpy as jnp
from jax import lax
from jax.experimental import pallas as pl
from jax.experimental.pallas import tpu as pltpu
from jax.sharding import PartitionSpec as P

MESH = pl.DeviceIdType.MESH
F32, BF16 = jnp.float32, jnp.bfloat16
ROWS, WIDTH, LABELS, SKEL, LEAF = 512, 768, 64, 256, 256
MSG = 72
CHUNKS = (32, 32, 32, 32, 64, 64, 128, 128)
BETA = 25.0 * math.log2(math.e)


def dot_nt(a, b):
    return lax.dot_general(a, b, (((1,), (1,)), ((), ())), preferred_element_type=F32)


def dot_nn(a, b):
    return jnp.dot(a, b, preferred_element_type=F32)


def split(value):
    high = value.astype(BF16)
    return high, (value - high.astype(F32)).astype(BF16)


def kernel(x_ref, lab_ref, skel_ref, urow_ref, near_ref, flocal_ref, fupper_ref, out_ref,
           pts, hi, lo, ncol, nrow, rt, masks, kown, scol, srow,
           contr, contr_in, part, land1, mid, land2, uq,
           up, uphi, uplo, upnrow,
           wp, wp_in, wpart, wland1, wmid, wland2, upw, kf_hi, kf_lo, kn_hi, kn_lo,
           acc, ret_out, ret_in,
           own_sem, s_sem, r_sem):
    gx, gy = lax.axis_index("gx"), lax.axis_index("gy")
    c, j = lax.div(gy, 2), lax.rem(gy, 2)
    y, z = lax.div(gx, 4), lax.rem(gx, 4)
    half = lax.div(c, 2)
    other = 1 - j
    crossed = lax.rem(j + half, 2)
    before, after = lax.rem(c + 3, 4), lax.rem(c + 1, 4)

    def chip(step, core):
        return (gx, lax.rem(c + step, 4) * 2 + core)

    sib = (gx, c * 2 + other)

    def y_peer(step):
        return (lax.rem(y + step, 4) * 4 + z, gy)

    def z_peer(step):
        return (y * 4 + lax.rem(z + step, 4), gy)

    own_copies = [pltpu.make_async_copy(x_ref.at[pl.ds(256 * leaf, 256)], pts.at[leaf], own_sem.at[leaf])
                  for leaf in range(2)]
    own_copies.append(pltpu.make_async_copy(lab_ref, rt.at[0, 0, 0:64], own_sem.at[2]))
    for copy in own_copies:
        copy.start()

    partners = [sib] + [chip(s, k) for s in (1, 3) for k in (j, other)]
    partners += [y_peer(s) for s in (1, 2, 3)] + [z_peer(s) for s in (1, 2, 3)]
    barrier = pltpu.get_barrier_semaphore()
    for partner in partners:
        pl.semaphore_signal(barrier, inc=1, device_id=partner, device_id_type=MESH)

    skel_t = jnp.where(lax.broadcasted_iota(jnp.int32, (ROWS, SKEL), 0) == skel_ref[...], 1.0, 0.0)
    scol[...] = jnp.broadcast_to(jnp.max(skel_t, axis=1, keepdims=True), (ROWS, 128))
    skel = jnp.transpose(skel_t)
    srow[...] = jnp.broadcast_to(jnp.sum(skel, axis=0, keepdims=True), (8, ROWS))
    chosen_t = jnp.where(
        lax.broadcasted_iota(jnp.int32, (SKEL, SKEL), 0) + gy * SKEL == urow_ref[...], 1.0, 0.0)
    chosen = jnp.transpose(chosen_t).astype(BF16)
    select = dot_nn(chosen, skel.astype(BF16)).astype(BF16)

    def prep(leaf):
        value = pts[leaf]
        high, low = split(value)
        hi[leaf] = high
        lo[leaf] = low
        wide = jnp.broadcast_to(jnp.sum(value * value, axis=1, keepdims=True) * BETA, (256, 128))
        ncol[leaf] = wide
        nrow[leaf] = jnp.transpose(wide)[0:8, :]

    for leaf in range(2):
        own_copies[leaf].wait()
        prep(leaf)

    rows_mine = jnp.zeros((SKEL, WIDTH), F32)
    for leaf in range(2):
        chosen_rows = select[:, 256 * leaf:256 * leaf + 256]
        rows_mine += dot_nn(chosen_rows, hi[leaf]) + dot_nn(chosen_rows, lo[leaf])
    for q in range(4):
        for h in range(2):
            contr[q, h] = rows_mine[64 * q + 32 * h:64 * q + 32 * h + 32, :]

    pl.semaphore_wait(barrier, len(partners))

    started = []

    def send(src, dst, device):
        at = len(started)
        copy = pltpu.make_async_remote_copy(
            src_ref=src, dst_ref=dst, send_sem=s_sem.at[at], recv_sem=r_sem.at[at],
            device_id=device, device_id_type=MESH)
        copy.start()
        started.append(copy)
        return copy

    def finish(copies):
        for copy in copies:
            copy.wait_recv()

    nodes = [gy, c * 2 + other, before * 2 + j, after * 2 + crossed]
    to_after, to_before = chip(1, j), chip(3, lax.rem(j + lax.div(before, 2), 2))

    bulk = {1: [], 3: []}

    def send_bulk(count=1):
        for _ in range(count):
            at = len(bulk[1])
            first, size = sum(CHUNKS[:at]), CHUNKS[at]
            leaf, rows = first // 256, pl.ds(first % 256, size)
            src = x_ref.at[pl.ds(first, size)]
            bulk[1].append(send(src, pts.at[4 + 2 * leaf, rows], to_after))
            bulk[3].append(send(src, pts.at[5 + 2 * leaf, rows], to_before))

    contr_msg = send(contr.at[:, other], contr_in, sib)
    label_msgs = [send(lab_ref, rt.at[slot, 0, 0:64], device)
                  for slot, device in ((2, to_after), (3, to_before), (1, sib))]
    send_bulk()
    sib_points = [send(x_ref.at[pl.ds(256 * leaf, 256)], pts.at[2 + leaf], sib) for leaf in range(2)]

    def many(parts, axis):
        return parts[0] if len(parts) == 1 else jnp.concatenate(parts, axis=axis)

    def affine(targets, sources):
        t_hi, t_lo, t_col = targets
        s_hi, s_lo, s_row = sources
        cross = dot_nt(t_hi, s_hi) + dot_nt(t_hi, s_lo) + dot_nt(t_lo, s_hi)
        wide = jnp.concatenate([t_col] * (s_hi.shape[0] // 128), axis=1)
        return jnp.exp2(cross * (2.0 * BETA) - wide - s_row)

    def as_targets(pieces):
        return (many([hi[l, f:f + n, :] for l, f, n in pieces], 0),
                many([lo[l, f:f + n, :] for l, f, n in pieces], 0),
                many([ncol[l, f:f + n, :] for l, f, n in pieces], 0))

    def as_sources(pieces):
        return (many([hi[l, f:f + n, :] for l, f, n in pieces], 0),
                many([lo[l, f:f + n, :] for l, f, n in pieces], 0),
                many([nrow[l, 0:1, f:f + n] for l, f, n in pieces], 1))

    def product_nt(k, rhs):
        k_hi, k_lo = split(k)
        r_hi, r_lo = split(rhs)
        both = dot_nt(k_hi, jnp.concatenate([r_hi, r_lo], axis=0))
        return both[:, :128] + both[:, 128:] + dot_nt(k_lo, r_hi)

    def product_nn(k_hi, k_lo, rhs):
        r_hi, r_lo = split(rhs)
        both = dot_nn(k_hi, jnp.concatenate([r_hi, r_lo], axis=1))
        return both[:, :128] + both[:, 128:] + dot_nn(k_lo, r_hi)

    lane = lax.broadcasted_iota(jnp.int32, (1, 128), 1)

    def pick(slot, row, at):
        return jnp.sum(jnp.where(lane == at, masks[slot, row:row + 1, :], 0.0), axis=1, keepdims=True)

    def near_rhs(slot, t, sources):
        return many([pick(slot, t, 2 * node + s) * rt[sl, 0, :, 256 * s + f:256 * s + f + n]
                     + pick(slot, 2, node) * rt[sl, 1, :, 256 * s + f:256 * s + f + n]
                     for sl, node, s, f, n in sources], 1)

    def near(target, slot, targets, source_pieces, source_terms):
        k = affine(as_targets([(l, f, n) for l, _, f, n in targets]), as_sources(source_pieces))
        at = 0
        for _, t, f, n in targets:
            acc[target, 256 * t + f:256 * t + f + n, :] += product_nt(
                k[at:at + n], near_rhs(slot, t, source_terms))
            at += n

    OWN = [(0, 0, 0, 256), (1, 1, 0, 256)]

    def up_sources(q, m):
        rows = pl.ds(pl.multiple_of((q * 4 + m) * 256, 256), 256)
        return uphi[rows, :], uplo[rows, :], upnrow[q * 4 + m, 0:1, :]

    def up_pair(parts):
        loaded = [up_sources(q, m) for q, m in parts]
        return (many([p[0] for p in loaded], 0), many([p[1] for p in loaded], 0), many([p[2] for p in loaded], 1))

    def up_rhs(slot, q, m):
        weights = upw[q, m]
        parts = []
        for n in range(4):
            cluster = n * 4 + m if q == 0 else m * 4 + n
            parts.append(weights[n].reshape(64, 128) * pick(slot, 3, cluster))
        return jnp.concatenate(parts, axis=0)

    acc[...] = jnp.zeros_like(acc)

    for slot in range(4):
        rt[slot, 0, 64:128, :] = jnp.where(
            lax.broadcasted_iota(jnp.int32, (64, ROWS), 0) == 0, 1.0, 0.0)
        rt[slot, 1, 72:128, :] = jnp.zeros((56, ROWS), F32)


    def mask_row(entries):
        row = jnp.zeros((1, 128), F32)
        for entry in entries:
            row += jnp.where(lane == entry, 1.0, 0.0)
        return row

    for t in range(2):
        masks[0, t:t + 1, :] = mask_row([near_ref[t, e] - gx * 16 for e in range(8)])
    masks[0, 2:3, :] = mask_row([flocal_ref[0, e] for e in range(7)])
    masks[0, 3:4, :] = mask_row([fupper_ref[0, e] for e in range(15)])
    masks[0, 4:8, :] = jnp.zeros((4, 128), F32)
    mask_msgs = [send(masks.at[0], masks.at[slot], device)
                 for slot, device in ((1, sib), (2, to_after), (3, to_before))]

    def chip_sum(mine, incoming, total):
        for q in range(4):
            total[q] = mine[q, j] + incoming[q]

    def round_one(total, land):
        return [send(total.at[lax.rem(c + 3, 4)], land.at[0], chip(3, j)),
                send(total.at[lax.rem(c + 2, 4)], land.at[1], chip(1, j))]

    def round_two(total, land, middle, land_two):
        middle[0] = total[c] + land[0]
        middle[1] = total[after] + land[1]
        return [send(middle.at[0], land_two.at[1], chip(3, j)),
                send(middle.at[1], land_two.at[0], chip(1, j))]

    contr_msg.wait_recv()
    chip_sum(contr, contr_in, part)
    ones = round_one(part, land1)
    send_bulk()

    kown[...] = affine(as_targets([(0, 0, 256), (1, 0, 256)]), as_sources([(0, 0, 256), (1, 0, 256)]))
    own_copies[2].wait()
    inverse = 1.0 / jnp.sum(kown[...] * scol[:, 0:1], axis=0, keepdims=True)
    lower = product_nt(kown[...] * inverse, rt[0, 0]) * scol[...]

    finish(ones)
    twos = round_two(part, land1, mid, land2)
    send_bulk()

    rt[0, 1] = jnp.transpose(lower)

    rows_at = lax.broadcasted_iota(jnp.int32, (256, ROWS), 0)
    cols_at = lax.broadcasted_iota(jnp.int32, (256, ROWS), 1)
    for t in range(2):
        k = jnp.where(rows_at + 256 * t == cols_at, 0.0, kown[256 * t:256 * t + 256, :])
        acc[0, 256 * t:256 * t + 256, :] += product_nt(
            k, near_rhs(0, t, [(0, gy, 0, 0, 256), (0, gy, 1, 0, 256)]))

    finish(twos)
    quarter0 = mid[0] + land2[0]
    quarter1 = mid[1] + land2[1]
    uq[c, j] = quarter0
    uq[after, j] = quarter1
    up[0, z, y, j] = quarter0
    up[1, y, z, j] = quarter1
    threes = [send(uq.at[after, j], uq.at[after, j], chip(3, j)),
              send(uq.at[c, j], uq.at[c, j], chip(1, j))]

    def phase_one(buffer):
        return ([send(buffer.at[0, z, y, j], buffer.at[0, z, y, j], y_peer(s)) for s in (1, 3, 2)]
                + [send(buffer.at[1, y, z, j], buffer.at[1, y, z, j], z_peer(s)) for s in (1, 3, 2)])

    def phase_two(buffer):
        return {s: [send(buffer.at[0, z, :, j], buffer.at[0, z, :, j], z_peer(s)),
                    send(buffer.at[1, y, :, j], buffer.at[1, y, :, j], y_peer(s))] for s in (1, 3, 2)}

    def majors(step):
        return lax.rem(z + 4 - step, 4), lax.rem(y + 4 - step, 4)

    def share_step(buffer, step):
        m0, m1 = majors(step)
        return [send(buffer.at[0, m0, :, j], buffer.at[0, m0, :, j], sib),
                send(buffer.at[1, m1, :, j], buffer.at[1, m1, :, j], sib)]

    up_one = phase_one(up)
    send_bulk()
    weight_msgs = [send(rt.at[0, 1, 0:MSG], rt.at[slot, 1, 0:MSG], device)
                   for slot, device in ((1, sib), (2, to_after), (3, to_before))]

    finish(sib_points)
    label_msgs[2].wait_recv()
    mask_msgs[0].wait_recv()
    for leaf in range(2):
        prep(2 + leaf)

    finish(up_one)
    up_two = phase_two(up)
    up_share = {0: share_step(up, 0)}

    finish(threes)
    share = send(uq.at[:, j], uq.at[:, j], sib)
    weight_msgs[0].wait_recv()
    near(0, 0, OWN, [(2, 0, 256), (3, 0, 256)], [(1, nodes[1], 0, 0, 256), (1, nodes[1], 1, 0, 256)])
    send_bulk()
    share.wait_recv()

    value = uq[...].reshape(SKEL, WIDTH)
    u_hi, u_lo = split(value)
    u_col = jnp.broadcast_to(jnp.sum(value * value, axis=1, keepdims=True) * BETA, (SKEL, 128))
    k = affine((u_hi, u_lo, u_col), as_sources([(0, 0, 256), (1, 0, 256)]))
    total = jnp.sum(k, axis=0, keepdims=True)
    shares = k * jnp.where(srow[0:1, :] > 0.0, 1.0 / total, 0.0)
    partial_sum = product_nt(shares, rt[0, 1])
    for q in range(4):
        for h in range(2):
            wp[q, h] = partial_sum[64 * q + 32 * h:64 * q + 32 * h + 32, :]
    wp_msg = send(wp.at[:, other], wp_in, sib)

    def prep_up(q, m):
        value = up[q, m].reshape(256, WIDTH)
        rows = pl.ds(pl.multiple_of((q * 4 + m) * 256, 256), 256)
        high, low = split(value)
        uphi[rows, :] = high
        uplo[rows, :] = low
        wide = jnp.broadcast_to(jnp.sum(value * value, axis=1, keepdims=True) * BETA, (256, 128))
        upnrow[q * 4 + m] = jnp.transpose(wide)[0:8, :]

    def far_own(step):
        m0, m1 = majors(step)
        prep_up(0, m0)
        prep_up(1, m1)
        k_hi, k_lo = split(affine(as_targets([(0, 0, 256), (1, 0, 256)]), up_pair([(0, m0), (1, m1)])))
        kf_hi[step] = k_hi
        kf_lo[step] = k_lo

    finish(up_share[0])
    far_own(0)

    wp_msg.wait_recv()
    chip_sum(wp, wp_in, wpart)
    w_ones = round_one(wpart, wland1)
    send_bulk()

    finish(w_ones)
    w_twos = round_two(wpart, wland1, wmid, wland2)
    send_bulk(len(CHUNKS) - len(bulk[1]))

    finish(up_two[1])
    up_share[1] = share_step(up, 1)
    finish(up_two[3])
    up_share[3] = share_step(up, 3)

    finish(w_twos)
    upw[0, z, y, j] = wmid[0] + wland2[0]
    upw[1, y, z, j] = wmid[1] + wland2[1]
    w_up_one = phase_one(upw)

    finish(up_share[1])
    far_own(1)
    finish(up_share[3])
    far_own(3)

    taken = [0]

    def leaf_arrives(leaf):
        while taken[0] < len(CHUNKS) and sum(CHUNKS[:taken[0] + 1]) <= 256 * leaf + 256:
            bulk[1][taken[0]].wait_recv()
            bulk[3][taken[0]].wait_recv()
            taken[0] += 1
        for side in range(2):
            prep(4 + 2 * leaf + side)

    SIB = [(2, 0, 0, 256), (3, 1, 0, 256)]

    def from_leaf(target, slot, targets, leaf):
        near(target, slot, targets, [(4 + 2 * leaf, 0, 256), (5 + 2 * leaf, 0, 256)],
             [(2, nodes[2], leaf, 0, 256), (3, nodes[3], leaf, 0, 256)])

    finish(label_msgs[:2] + mask_msgs[1:] + weight_msgs[1:])
    leaf_arrives(0)
    from_leaf(0, 0, OWN, 0)
    from_leaf(3, 1, SIB, 0)

    finish(up_two[2])
    up_share[2] = share_step(up, 2)
    finish(w_up_one)
    w_up_two = phase_two(upw)
    finish(up_share[2])
    far_own(2)

    def far_kernel(leaf, q):
        return split(affine(as_targets([(leaf, 0, 256)]), up_pair([(q, m) for m in range(4)])))

    for side in range(2):
        kn_hi[side], kn_lo[side] = far_kernel(4 + side, 1 - side)

    for s in (1, 3, 2):
        finish(w_up_two[s])
    w_share = [send(upw.at[:, :, :, j], upw.at[:, :, :, j], sib)]
    finish(w_share)

    for step in range(4):
        m0, m1 = majors(step)
        rhs = jnp.concatenate([up_rhs(0, 0, m0), up_rhs(0, 1, m1)], axis=0)
        acc[0] += product_nn(kf_hi[step], kf_lo[step], rhs)

    def far_terms(side):
        return jnp.concatenate([up_rhs(2 + side, 1 - side, m) for m in range(4)], axis=0)

    for side in range(2):
        acc[1 + side, 0:256, :] += product_nn(kn_hi[side], kn_lo[side], far_terms(side))

    leaf_arrives(1)
    backs = []
    for side in range(2):
        near(1 + side, 2 + side, [(4 + side, 0, 0, 256), (6 + side, 1, 0, 256)],
             [(5 - side, 0, 256), (7 - side, 0, 256)],
             [(3 - side, nodes[3 - side], 0, 0, 256), (3 - side, nodes[3 - side], 1, 0, 256)])
        k_hi, k_lo = far_kernel(6 + side, 1 - side)
        acc[1 + side, 256:512, :] += product_nn(k_hi, k_lo, far_terms(side))
        ret_out[side] = jnp.transpose(acc[1 + side])
        backs.append(send(ret_out.at[side, 0:MSG], ret_in.at[side, 0:MSG],
                          chip(3, j) if side == 0 else chip(1, crossed)))
    from_leaf(3, 1, SIB, 1)
    ret_out[2] = jnp.transpose(acc[3])
    backs.append(send(ret_out.at[2, 0:MSG], ret_in.at[2, 0:MSG], sib))
    from_leaf(0, 0, OWN, 1)
    sums = jnp.transpose(acc[0])[0:MSG]
    for side in (2, 0, 1):
        backs[side].wait_recv()
        sums += ret_in[side, 0:MSG]
    out_ref[...] = sums[0:LABELS] / sums[LABELS:LABELS + 1]

    for copy in started:
        copy.wait_send()


N_COPIES = 110


def on_device(points, labels, skeleton_rows, upper_rows, near_list, far_local, far_upper):
    vmem = pl.BlockSpec(memory_space=pltpu.VMEM)
    smem = pl.BlockSpec(memory_space=pltpu.SMEM)
    hbm = pl.BlockSpec(memory_space=pl.ANY)
    result = pl.pallas_call(
        kernel,
        out_shape=jax.ShapeDtypeStruct((LABELS, ROWS), F32),
        in_specs=[hbm, hbm, vmem, vmem, smem, smem, smem],
        out_specs=vmem,
        scratch_shapes=[
            pltpu.VMEM((8, LEAF, WIDTH), F32),
            pltpu.VMEM((8, LEAF, WIDTH), BF16),
            pltpu.VMEM((8, LEAF, WIDTH), BF16),
            pltpu.VMEM((8, LEAF, 128), F32),
            pltpu.VMEM((8, 8, LEAF), F32),
            pltpu.VMEM((4, 2, 128, ROWS), F32),
            pltpu.VMEM((4, 8, 128), F32),
            pltpu.VMEM((ROWS, ROWS), F32),
            pltpu.VMEM((ROWS, 128), F32),
            pltpu.VMEM((8, ROWS), F32),
            pltpu.VMEM((4, 2, 32, WIDTH), F32),
            pltpu.VMEM((4, 32, WIDTH), F32),
            pltpu.VMEM((4, 32, WIDTH), F32),
            pltpu.VMEM((2, 32, WIDTH), F32),
            pltpu.VMEM((2, 32, WIDTH), F32),
            pltpu.VMEM((2, 32, WIDTH), F32),
            pltpu.VMEM((4, 2, 32, WIDTH), F32),
            pltpu.VMEM((2, 4, 4, 2, 32, WIDTH), F32),
            pltpu.VMEM((2048, WIDTH), BF16),
            pltpu.VMEM((2048, WIDTH), BF16),
            pltpu.VMEM((8, 8, 256), F32),
            pltpu.VMEM((4, 2, 32, 128), F32),
            pltpu.VMEM((4, 32, 128), F32),
            pltpu.VMEM((4, 32, 128), F32),
            pltpu.VMEM((2, 32, 128), F32),
            pltpu.VMEM((2, 32, 128), F32),
            pltpu.VMEM((2, 32, 128), F32),
            pltpu.VMEM((2, 4, 4, 2, 32, 128), F32),
            pltpu.VMEM((4, ROWS, ROWS), BF16),
            pltpu.VMEM((4, ROWS, ROWS), BF16),
            pltpu.VMEM((2, LEAF, 1024), BF16),
            pltpu.VMEM((2, LEAF, 1024), BF16),
            pltpu.VMEM((4, ROWS, 128), F32),
            pltpu.VMEM((3, 128, ROWS), F32),
            pltpu.VMEM((3, 128, ROWS), F32),
            pltpu.SemaphoreType.DMA((3,)),
            pltpu.SemaphoreType.DMA((N_COPIES,)),
            pltpu.SemaphoreType.DMA((N_COPIES,)),
        ],
        compiler_params=pltpu.CompilerParams(
            collective_id=0, has_side_effects=True, vmem_limit_bytes=62 * 1024 * 1024),
        cost_estimate=pl.CostEstimate(
            flops=64 * 6 * 256 * 256 * 768, bytes_accessed=2 * 1024 * 1024, transcendentals=64 * 256 * 256),
    )(points, labels.T, skeleton_rows, upper_rows, near_list, far_local, far_upper)
    return result.T


def solution(mesh):
    return jax.shard_map(
        on_device,
        mesh=mesh,
        in_specs=(
            P(("gx", "gy"), None),
            P(("gx", "gy"), None),
            P(("gx", "gy"), None),
            P("gx", None),
            P(("gx", "gy"), None),
            P(("gx", "gy"), None),
            P(("gx", "gy"), None),
        ),
        out_specs=P(("gx", "gy"), None),
        check_vma=False,
    )
```

```python
import functools
import math

import jax
import jax.numpy as jnp
from jax import lax
from jax.experimental import pallas as pl
from jax.experimental.pallas import tpu as pltpu
from jax.sharding import PartitionSpec as P

MESH = pl.DeviceIdType.MESH
F32, BF16 = jnp.float32, jnp.bfloat16
ROWS, WIDTH, LABELS, SKEL, LEAF = 512, 768, 64, 256, 256
MSG = 72
CHUNKS = (32, 32, 32, 32, 64, 32, 32, 64, 64, 128)
BETA = 25.0 * math.log2(math.e)


def dot_nt(a, b):
    return lax.dot_general(a, b, (((1,), (1,)), ((), ())), preferred_element_type=F32)


def dot_nn(a, b):
    return jnp.dot(a, b, preferred_element_type=F32)


def split(value):
    high = value.astype(BF16)
    return high, (value - high.astype(F32)).astype(BF16)


def kernel(x_ref, lab_ref, skel_hbm, urow_hbm, near_hbm, flocal_hbm, fupper_hbm, out_ref,
           skel_ref, urow_ref, near_ref, flocal_ref, fupper_ref,
           pts, hi, lo, ncol, nrow, rt, masks, kown, scol, srow,
           contr, contr_in, part, land1, mid, land2, uq,
           up, uphi, uplo, upnrow,
           wp, wp_in, wpart, wland1, wmid, wland2, upw, kf_hi, kf_lo, kn_hi, kn_lo,
           acc, ret_out, ret_in,
           own_sem, s_sem, r_sem):
    gx, gy = lax.axis_index("gx"), lax.axis_index("gy")
    c, j = lax.div(gy, 2), lax.rem(gy, 2)
    y, z = lax.div(gx, 4), lax.rem(gx, 4)
    half = lax.div(c, 2)
    other = 1 - j
    crossed = lax.rem(j + half, 2)
    before, after = lax.rem(c + 3, 4), lax.rem(c + 1, 4)

    def chip(step, core):
        return (gx, lax.rem(c + step, 4) * 2 + core)

    sib = (gx, c * 2 + other)

    def y_peer(step):
        return (lax.rem(y + step, 4) * 4 + z, gy)

    def z_peer(step):
        return (y * 4 + lax.rem(z + step, 4), gy)

    own_copies = [pltpu.make_async_copy(x_ref.at[pl.ds(256 * leaf, 256)], pts.at[leaf], own_sem.at[leaf])
                  for leaf in range(2)]
    own_copies.append(pltpu.make_async_copy(lab_ref, rt.at[0, 0, 0:64], own_sem.at[2]))
    small = ((skel_hbm, skel_ref), (urow_hbm, urow_ref), (near_hbm, near_ref),
             (flocal_hbm, flocal_ref), (fupper_hbm, fupper_ref))
    own_copies += [pltpu.make_async_copy(src, dst, own_sem.at[3 + at]) for at, (src, dst) in enumerate(small)]
    for copy in own_copies[3:] + own_copies[:3]:
        copy.start()

    partners = [sib] + [chip(s, k) for s in (1, 3) for k in (j, other)]
    partners += [y_peer(s) for s in (1, 2, 3)] + [z_peer(s) for s in (1, 2, 3)]
    barrier = pltpu.get_barrier_semaphore()
    for partner in partners:
        pl.semaphore_signal(barrier, inc=1, device_id=partner, device_id_type=MESH)

    own_copies[3].wait()
    own_copies[4].wait()
    skel_t = jnp.where(lax.broadcasted_iota(jnp.int32, (ROWS, SKEL), 0) == skel_ref[...], 1.0, 0.0)
    scol[...] = jnp.broadcast_to(jnp.max(skel_t, axis=1, keepdims=True), (ROWS, 128))
    skel = jnp.transpose(skel_t)
    srow[...] = jnp.broadcast_to(jnp.sum(skel, axis=0, keepdims=True), (8, ROWS))
    chosen_t = jnp.where(
        lax.broadcasted_iota(jnp.int32, (SKEL, SKEL), 0) + gy * SKEL == urow_ref[...], 1.0, 0.0)
    chosen = jnp.transpose(chosen_t).astype(BF16)
    select = dot_nn(chosen, skel.astype(BF16)).astype(BF16)

    def prep(leaf):
        value = pts[leaf]
        high, low = split(value)
        hi[leaf] = high
        lo[leaf] = low
        wide = jnp.broadcast_to(jnp.sum(value * value, axis=1, keepdims=True) * BETA, (256, 128))
        ncol[leaf] = wide
        nrow[leaf] = jnp.transpose(wide)[0:8, :]

    for leaf in range(2):
        own_copies[leaf].wait()
        prep(leaf)

    rows_mine = jnp.zeros((SKEL, WIDTH), F32)
    for leaf in range(2):
        chosen_rows = select[:, 256 * leaf:256 * leaf + 256]
        rows_mine += dot_nn(chosen_rows, hi[leaf]) + dot_nn(chosen_rows, lo[leaf])
    for q in range(4):
        for h in range(2):
            contr[q, h] = rows_mine[64 * q + 32 * h:64 * q + 32 * h + 32, :]

    pl.semaphore_wait(barrier, len(partners))

    started = []

    def send(src, dst, device):
        at = len(started)
        copy = pltpu.make_async_remote_copy(
            src_ref=src, dst_ref=dst, send_sem=s_sem.at[at], recv_sem=r_sem.at[at],
            device_id=device, device_id_type=MESH)
        copy.start()
        started.append(copy)
        return copy

    def finish(copies):
        for copy in copies:
            copy.wait_recv()

    nodes = [gy, c * 2 + other, before * 2 + j, after * 2 + crossed]
    to_after, to_before = chip(1, j), chip(3, lax.rem(j + lax.div(before, 2), 2))

    bulk = {1: [], 3: []}

    def send_bulk(count=1):
        for _ in range(count):
            at = len(bulk[1])
            first, size = sum(CHUNKS[:at]), CHUNKS[at]
            leaf, rows = first // 256, pl.ds(first % 256, size)
            src = x_ref.at[pl.ds(first, size)]
            bulk[1].append(send(src, pts.at[4 + 2 * leaf, rows], to_after))
            bulk[3].append(send(src, pts.at[5 + 2 * leaf, rows], to_before))

    contr_msg = send(contr.at[:, other], contr_in, sib)
    label_msgs = [send(lab_ref, rt.at[slot, 0, 0:64], device)
                  for slot, device in ((2, to_after), (3, to_before), (1, sib))]
    send_bulk()
    sib_points = [send(x_ref.at[pl.ds(256 * leaf, 256)], pts.at[2 + leaf], sib) for leaf in range(2)]

    def many(parts, axis):
        return parts[0] if len(parts) == 1 else jnp.concatenate(parts, axis=axis)

    def affine(targets, sources):
        t_hi, t_lo, t_col = targets
        s_hi, s_lo, s_row = sources
        cross = dot_nt(t_hi, s_hi) + dot_nt(t_hi, s_lo) + dot_nt(t_lo, s_hi)
        wide = jnp.concatenate([t_col] * (s_hi.shape[0] // 128), axis=1)
        return jnp.exp2(cross * (2.0 * BETA) - wide - s_row)

    def as_targets(pieces):
        return (many([hi[l, f:f + n, :] for l, f, n in pieces], 0),
                many([lo[l, f:f + n, :] for l, f, n in pieces], 0),
                many([ncol[l, f:f + n, :] for l, f, n in pieces], 0))

    def as_sources(pieces):
        return (many([hi[l, f:f + n, :] for l, f, n in pieces], 0),
                many([lo[l, f:f + n, :] for l, f, n in pieces], 0),
                many([nrow[l, 0:1, f:f + n] for l, f, n in pieces], 1))

    def product_nt(k, rhs):
        k_hi, k_lo = split(k)
        r_hi, r_lo = split(rhs)
        both = dot_nt(k_hi, jnp.concatenate([r_hi, r_lo], axis=0))
        return both[:, :128] + both[:, 128:] + dot_nt(k_lo, r_hi)

    def product_nn(k_hi, k_lo, rhs):
        r_hi, r_lo = split(rhs)
        both = dot_nn(k_hi, jnp.concatenate([r_hi, r_lo], axis=1))
        return both[:, :128] + both[:, 128:] + dot_nn(k_lo, r_hi)

    lane = lax.broadcasted_iota(jnp.int32, (1, 128), 1)

    def pick(slot, row, at):
        return jnp.sum(jnp.where(lane == at, masks[slot, row:row + 1, :], 0.0), axis=1, keepdims=True)

    def near_rhs(slot, t, sources):
        return many([pick(slot, t, 2 * node + s) * rt[sl, 0, :, 256 * s + f:256 * s + f + n]
                     + pick(slot, 2, node) * rt[sl, 1, :, 256 * s + f:256 * s + f + n]
                     for sl, node, s, f, n in sources], 1)

    def near(target, slot, targets, source_pieces, source_terms):
        k = affine(as_targets([(l, f, n) for l, _, f, n in targets]), as_sources(source_pieces))
        at = 0
        for _, t, f, n in targets:
            acc[target, 256 * t + f:256 * t + f + n, :] += product_nt(
                k[at:at + n], near_rhs(slot, t, source_terms))
            at += n

    OWN = [(0, 0, 0, 256), (1, 1, 0, 256)]

    def up_sources(q, m):
        rows = pl.ds(pl.multiple_of((q * 4 + m) * 256, 256), 256)
        return uphi[rows, :], uplo[rows, :], upnrow[q * 4 + m, 0:1, :]

    def up_pair(parts):
        loaded = [up_sources(q, m) for q, m in parts]
        return (many([p[0] for p in loaded], 0), many([p[1] for p in loaded], 0), many([p[2] for p in loaded], 1))

    def up_rhs(slot, q, m):
        weights = upw[q, m]
        parts = []
        for n in range(4):
            cluster = n * 4 + m if q == 0 else m * 4 + n
            parts.append(weights[n].reshape(64, 128) * pick(slot, 3, cluster))
        return jnp.concatenate(parts, axis=0)

    acc[...] = jnp.zeros_like(acc)

    for slot in range(4):
        rt[slot, 0, 64:128, :] = jnp.where(
            lax.broadcasted_iota(jnp.int32, (64, ROWS), 0) == 0, 1.0, 0.0)
        rt[slot, 1, 72:128, :] = jnp.zeros((56, ROWS), F32)


    for copy in own_copies[5:]:
        copy.wait()
    def mask_row(entries):
        row = jnp.zeros((1, 128), F32)
        for entry in entries:
            row += jnp.where(lane == entry, 1.0, 0.0)
        return row

    for t in range(2):
        masks[0, t:t + 1, :] = mask_row([near_ref[t, e] - gx * 16 for e in range(8)])
    masks[0, 2:3, :] = mask_row([flocal_ref[0, e] for e in range(7)])
    masks[0, 3:4, :] = mask_row([fupper_ref[0, e] for e in range(15)])
    masks[0, 4:8, :] = jnp.zeros((4, 128), F32)
    mask_msgs = [send(masks.at[0], masks.at[slot], device)
                 for slot, device in ((1, sib), (2, to_after), (3, to_before))]

    def chip_sum(mine, incoming, total):
        for q in range(4):
            total[q] = mine[q, j] + incoming[q]

    def round_one(total, land):
        return [send(total.at[lax.rem(c + 3, 4)], land.at[0], chip(3, j)),
                send(total.at[lax.rem(c + 2, 4)], land.at[1], chip(1, j))]

    def round_two(total, land, middle, land_two):
        middle[0] = total[c] + land[0]
        middle[1] = total[after] + land[1]
        return [send(middle.at[0], land_two.at[1], chip(3, j)),
                send(middle.at[1], land_two.at[0], chip(1, j))]

    contr_msg.wait_recv()
    chip_sum(contr, contr_in, part)
    ones = round_one(part, land1)
    send_bulk()

    kown[...] = affine(as_targets([(0, 0, 256), (1, 0, 256)]), as_sources([(0, 0, 256), (1, 0, 256)]))
    own_copies[2].wait()
    inverse = 1.0 / jnp.sum(kown[...] * scol[:, 0:1], axis=0, keepdims=True)
    lower = product_nt(kown[...] * inverse, rt[0, 0]) * scol[...]

    finish(ones)
    twos = round_two(part, land1, mid, land2)
    send_bulk()

    rt[0, 1] = jnp.transpose(lower)

    rows_at = lax.broadcasted_iota(jnp.int32, (256, ROWS), 0)
    cols_at = lax.broadcasted_iota(jnp.int32, (256, ROWS), 1)
    for t in range(2):
        k = jnp.where(rows_at + 256 * t == cols_at, 0.0, kown[256 * t:256 * t + 256, :])
        acc[0, 256 * t:256 * t + 256, :] += product_nt(
            k, near_rhs(0, t, [(0, gy, 0, 0, 256), (0, gy, 1, 0, 256)]))

    finish(twos)
    quarter0 = mid[0] + land2[0]
    quarter1 = mid[1] + land2[1]
    uq[c, j] = quarter0
    uq[after, j] = quarter1
    up[0, z, y, j] = quarter0
    up[1, y, z, j] = quarter1
    threes = [send(uq.at[after, j], uq.at[after, j], chip(3, j)),
              send(uq.at[c, j], uq.at[c, j], chip(1, j))]

    def phase_one(buffer):
        return ([send(buffer.at[0, z, y, j], buffer.at[0, z, y, j], y_peer(s)) for s in (1, 3, 2)]
                + [send(buffer.at[1, y, z, j], buffer.at[1, y, z, j], z_peer(s)) for s in (1, 3, 2)])

    def phase_two(buffer):
        return {s: [send(buffer.at[0, z, :, j], buffer.at[0, z, :, j], z_peer(s)),
                    send(buffer.at[1, y, :, j], buffer.at[1, y, :, j], y_peer(s))] for s in (1, 3)}

    def pass_on(buffer):
        copies = []
        for step, rows in ((1, slice(0, 2)), (3, slice(2, 4))):
            m0, m1 = majors(step)
            copies += [send(buffer.at[0, m0, rows, j], buffer.at[0, m0, rows, j], z_peer(step)),
                       send(buffer.at[1, m1, rows, j], buffer.at[1, m1, rows, j], y_peer(step))]
        return copies

    def majors(step):
        return lax.rem(z + 4 - step, 4), lax.rem(y + 4 - step, 4)

    def share_step(buffer, step):
        m0, m1 = majors(step)
        return [send(buffer.at[0, m0, :, j], buffer.at[0, m0, :, j], sib),
                send(buffer.at[1, m1, :, j], buffer.at[1, m1, :, j], sib)]

    up_one = phase_one(up)
    send_bulk()
    weight_msgs = [send(rt.at[0, 1, 0:MSG], rt.at[slot, 1, 0:MSG], device)
                   for slot, device in ((1, sib), (2, to_after), (3, to_before))]

    send_bulk()

    finish(sib_points)
    label_msgs[2].wait_recv()
    mask_msgs[0].wait_recv()
    for leaf in range(2):
        prep(2 + leaf)

    finish(up_one)
    up_two = phase_two(up)
    up_share = {0: share_step(up, 0)}

    finish(threes)
    share = send(uq.at[:, j], uq.at[:, j], sib)
    weight_msgs[0].wait_recv()
    near(0, 0, OWN, [(2, 0, 256), (3, 0, 256)], [(1, nodes[1], 0, 0, 256), (1, nodes[1], 1, 0, 256)])
    send_bulk()
    share.wait_recv()

    value = uq[...].reshape(SKEL, WIDTH)
    u_hi, u_lo = split(value)
    u_col = jnp.broadcast_to(jnp.sum(value * value, axis=1, keepdims=True) * BETA, (SKEL, 128))
    k = affine((u_hi, u_lo, u_col), as_sources([(0, 0, 256), (1, 0, 256)]))
    total = jnp.sum(k, axis=0, keepdims=True)
    shares = k * jnp.where(srow[0:1, :] > 0.0, 1.0 / total, 0.0)
    partial_sum = product_nt(shares, rt[0, 1])
    for q in range(4):
        for h in range(2):
            wp[q, h] = partial_sum[64 * q + 32 * h:64 * q + 32 * h + 32, :]
    wp_msg = send(wp.at[:, other], wp_in, sib)

    def prep_up(q, m):
        value = up[q, m].reshape(256, WIDTH)
        rows = pl.ds(pl.multiple_of((q * 4 + m) * 256, 256), 256)
        high, low = split(value)
        uphi[rows, :] = high
        uplo[rows, :] = low
        wide = jnp.broadcast_to(jnp.sum(value * value, axis=1, keepdims=True) * BETA, (256, 128))
        upnrow[q * 4 + m] = jnp.transpose(wide)[0:8, :]

    def far_own(step):
        m0, m1 = majors(step)
        prep_up(0, m0)
        prep_up(1, m1)
        k_hi, k_lo = split(affine(as_targets([(0, 0, 256), (1, 0, 256)]), up_pair([(0, m0), (1, m1)])))
        kf_hi[step] = k_hi
        kf_lo[step] = k_lo

    wp_msg.wait_recv()
    chip_sum(wp, wp_in, wpart)
    w_ones = round_one(wpart, wland1)
    send_bulk()
    finish(up_share[0])
    far_own(0)
    finish(w_ones)
    w_twos = round_two(wpart, wland1, wmid, wland2)
    send_bulk(len(CHUNKS) - len(bulk[1]))
    for step in (1, 3):
        finish(up_two[step])
    up_two[2] = pass_on(up)
    for step in (1, 3):
        up_share[step] = share_step(up, step)

    taken = [0]

    def leaf_arrives(leaf):
        while taken[0] < len(CHUNKS) and sum(CHUNKS[:taken[0] + 1]) <= 256 * leaf + 256:
            bulk[1][taken[0]].wait_recv()
            bulk[3][taken[0]].wait_recv()
            taken[0] += 1
        for side in range(2):
            prep(4 + 2 * leaf + side)

    SIB = [(2, 0, 0, 256), (3, 1, 0, 256)]

    def from_leaf(target, slot, targets, leaf):
        near(target, slot, targets, [(4 + 2 * leaf, 0, 256), (5 + 2 * leaf, 0, 256)],
             [(2, nodes[2], leaf, 0, 256), (3, nodes[3], leaf, 0, 256)])

    finish(label_msgs[:2] + mask_msgs[1:] + weight_msgs[1:])
    leaf_arrives(0)
    from_leaf(3, 1, SIB, 0)
    finish(w_twos)
    upw[0, z, y, j] = wmid[0] + wland2[0]
    upw[1, y, z, j] = wmid[1] + wland2[1]
    w_up_one = phase_one(upw)
    from_leaf(0, 0, OWN, 0)

    finish(up_two[2])
    up_share[2] = share_step(up, 2)
    finish(up_share[1])
    far_own(1)
    finish(w_up_one)
    w_up_two = phase_two(upw)
    finish(up_share[3])
    far_own(3)
    for step in (1, 3):
        finish(w_up_two[step])
    w_pass = pass_on(upw)
    finish(up_share[2])
    far_own(2)
    finish(w_pass)
    w_share = [send(upw.at[:, :, :, j], upw.at[:, :, :, j], sib)]

    def far_kernel(leaf, q):
        return split(affine(as_targets([(leaf, 0, 256)]), up_pair([(q, m) for m in range(4)])))

    for side in range(2):
        kn_hi[side], kn_lo[side] = far_kernel(4 + side, 1 - side)

    finish(w_share)

    for step in range(4):
        m0, m1 = majors(step)
        rhs = jnp.concatenate([up_rhs(0, 0, m0), up_rhs(0, 1, m1)], axis=0)
        acc[0] += product_nn(kf_hi[step], kf_lo[step], rhs)

    def far_terms(side):
        return jnp.concatenate([up_rhs(2 + side, 1 - side, m) for m in range(4)], axis=0)

    for side in range(2):
        acc[1 + side, 0:256, :] += product_nn(kn_hi[side], kn_lo[side], far_terms(side))

    leaf_arrives(1)
    both = [[(4 + side, 0, 256), (6 + side, 0, 256)] for side in range(2)]
    terms = [[(2 + side, nodes[2 + side], leaf, 0, 256) for leaf in range(2)] for side in range(2)]
    k_hi, k_lo = split(affine(as_targets(both[0]), as_sources(both[1])))
    turned = []
    for t in range(2):
        cols = slice(256 * t, 256 * t + 256)
        r_hi, r_lo = split(near_rhs(3, t, terms[0]))
        two = dot_nn(jnp.concatenate([r_hi, r_lo], axis=0), k_hi[:, cols])
        turned.append(two[:128] + two[128:] + dot_nn(r_hi, k_lo[:, cols]))
        rows = slice(256 * t, 256 * t + 256)
        r_hi, r_lo = split(near_rhs(2, t, terms[1]))
        two = dot_nt(k_hi[rows], jnp.concatenate([r_hi, r_lo], axis=0))
        acc[1, rows, :] += two[:, :128] + two[:, 128:] + dot_nt(k_lo[rows], r_hi)
    ret_out[1] = jnp.concatenate(turned, axis=1)
    backs = []
    for side in range(2):
        f_hi, f_lo = far_kernel(6 + side, 1 - side)
        acc[1 + side, 256:512, :] += product_nn(f_hi, f_lo, far_terms(side))
        done = jnp.transpose(acc[1 + side])
        ret_out[side] = done if side == 0 else ret_out[1] + done
        backs.append(send(ret_out.at[side, 0:MSG], ret_in.at[side, 0:MSG],
                          chip(3, j) if side == 0 else chip(1, crossed)))
    from_leaf(3, 1, SIB, 1)
    ret_out[2] = jnp.transpose(acc[3])
    backs.append(send(ret_out.at[2, 0:MSG], ret_in.at[2, 0:MSG], sib))
    from_leaf(0, 0, OWN, 1)
    sums = jnp.transpose(acc[0])[0:MSG]
    for side in (2, 0, 1):
        backs[side].wait_recv()
        sums += ret_in[side, 0:MSG]
    out_ref[...] = sums[0:LABELS] / sums[LABELS:LABELS + 1]

    for copy in started:
        copy.wait_send()


N_COPIES = 110


def on_device(points, labels, skeleton_rows, upper_rows, near_list, far_local, far_upper):
    vmem = pl.BlockSpec(memory_space=pltpu.VMEM)
    hbm = pl.BlockSpec(memory_space=pl.ANY)
    result = pl.pallas_call(
        kernel,
        out_shape=jax.ShapeDtypeStruct((LABELS, ROWS), F32),
        in_specs=[hbm] * 7,
        out_specs=vmem,
        scratch_shapes=[
            pltpu.VMEM(skeleton_rows.shape, jnp.int32),
            pltpu.VMEM(upper_rows.shape, jnp.int32),
            pltpu.SMEM(near_list.shape, jnp.int32),
            pltpu.SMEM(far_local.shape, jnp.int32),
            pltpu.SMEM(far_upper.shape, jnp.int32),
            pltpu.VMEM((8, LEAF, WIDTH), F32),
            pltpu.VMEM((8, LEAF, WIDTH), BF16),
            pltpu.VMEM((8, LEAF, WIDTH), BF16),
            pltpu.VMEM((8, LEAF, 128), F32),
            pltpu.VMEM((8, 8, LEAF), F32),
            pltpu.VMEM((4, 2, 128, ROWS), F32),
            pltpu.VMEM((4, 8, 128), F32),
            pltpu.VMEM((ROWS, ROWS), F32),
            pltpu.VMEM((ROWS, 128), F32),
            pltpu.VMEM((8, ROWS), F32),
            pltpu.VMEM((4, 2, 32, WIDTH), F32),
            pltpu.VMEM((4, 32, WIDTH), F32),
            pltpu.VMEM((4, 32, WIDTH), F32),
            pltpu.VMEM((2, 32, WIDTH), F32),
            pltpu.VMEM((2, 32, WIDTH), F32),
            pltpu.VMEM((2, 32, WIDTH), F32),
            pltpu.VMEM((4, 2, 32, WIDTH), F32),
            pltpu.VMEM((2, 4, 4, 2, 32, WIDTH), F32),
            pltpu.VMEM((2048, WIDTH), BF16),
            pltpu.VMEM((2048, WIDTH), BF16),
            pltpu.VMEM((8, 8, 256), F32),
            pltpu.VMEM((4, 2, 32, 128), F32),
            pltpu.VMEM((4, 32, 128), F32),
            pltpu.VMEM((4, 32, 128), F32),
            pltpu.VMEM((2, 32, 128), F32),
            pltpu.VMEM((2, 32, 128), F32),
            pltpu.VMEM((2, 32, 128), F32),
            pltpu.VMEM((2, 4, 4, 2, 32, 128), F32),
            pltpu.VMEM((4, ROWS, ROWS), BF16),
            pltpu.VMEM((4, ROWS, ROWS), BF16),
            pltpu.VMEM((2, LEAF, 1024), BF16),
            pltpu.VMEM((2, LEAF, 1024), BF16),
            pltpu.VMEM((4, ROWS, 128), F32),
            pltpu.VMEM((3, 128, ROWS), F32),
            pltpu.VMEM((3, 128, ROWS), F32),
            pltpu.SemaphoreType.DMA((8,)),
            pltpu.SemaphoreType.DMA((N_COPIES,)),
            pltpu.SemaphoreType.DMA((N_COPIES,)),
        ],
        compiler_params=pltpu.CompilerParams(
            collective_id=0, has_side_effects=True, vmem_limit_bytes=62 * 1024 * 1024),
        cost_estimate=pl.CostEstimate(
            flops=64 * 6 * 256 * 256 * 768, bytes_accessed=2 * 1024 * 1024, transcendentals=64 * 256 * 256),
    )(points, labels.T, skeleton_rows, upper_rows, near_list, far_local, far_upper)
    return result.T


def solution(mesh):
    return jax.shard_map(
        on_device,
        mesh=mesh,
        in_specs=(
            P(("gx", "gy"), None),
            P(("gx", "gy"), None),
            P(("gx", "gy"), None),
            P("gx", None),
            P(("gx", "gy"), None),
            P(("gx", "gy"), None),
            P(("gx", "gy"), None),
        ),
        out_specs=P(("gx", "gy"), None),
        check_vma=False,
    )
```

```python
import functools
import math

import jax
import jax.numpy as jnp
from jax import lax
from jax.experimental import pallas as pl
from jax.experimental.pallas import tpu as pltpu
from jax.sharding import PartitionSpec as P

MESH = pl.DeviceIdType.MESH
F32, BF16 = jnp.float32, jnp.bfloat16
ROWS, WIDTH, LABELS, SKEL, LEAF = 512, 768, 64, 256, 256
MSG = 72
CHUNKS = (32, 32, 32, 32, 48, 32, 48, 64, 64, 128)
BETA = 25.0 * math.log2(math.e)


def dot_nt(a, b):
    return lax.dot_general(a, b, (((1,), (1,)), ((), ())), preferred_element_type=F32)


def dot_nn(a, b):
    return jnp.dot(a, b, preferred_element_type=F32)


def split(value):
    high = value.astype(BF16)
    return high, (value - high.astype(F32)).astype(BF16)


def kernel(x_ref, lab_ref, skel_hbm, urow_hbm, near_hbm, flocal_hbm, fupper_hbm, out_ref,
           skel_ref, urow_ref, near_ref, flocal_ref, fupper_ref,
           pts, hi, lo, ncol, nrow, rt, masks, kown, scol, srow,
           contr, contr_in, part, land1, mid, land2, uq,
           up, uphi, uplo, upnrow,
           wp, wp_in, wpart, wland1, wmid, wland2, upw, kf_hi, kf_lo, kn_hi, kn_lo,
           acc, ret_out, ret_in,
           own_sem, s_sem, r_sem):
    gx, gy = lax.axis_index("gx"), lax.axis_index("gy")
    c, j = lax.div(gy, 2), lax.rem(gy, 2)
    y, z = lax.div(gx, 4), lax.rem(gx, 4)
    half = lax.div(c, 2)
    other = 1 - j
    crossed = lax.rem(j + half, 2)
    before, after = lax.rem(c + 3, 4), lax.rem(c + 1, 4)

    def chip(step, core):
        return (gx, lax.rem(c + step, 4) * 2 + core)

    sib = (gx, c * 2 + other)

    def y_peer(step):
        return (lax.rem(y + step, 4) * 4 + z, gy)

    def z_peer(step):
        return (y * 4 + lax.rem(z + step, 4), gy)

    own_copies = [pltpu.make_async_copy(x_ref.at[pl.ds(256 * leaf, 256)], pts.at[leaf], own_sem.at[leaf])
                  for leaf in range(2)]
    own_copies.append(pltpu.make_async_copy(lab_ref, rt.at[0, 0, 0:64], own_sem.at[2]))
    small = ((skel_hbm, skel_ref), (urow_hbm, urow_ref), (near_hbm, near_ref),
             (flocal_hbm, flocal_ref), (fupper_hbm, fupper_ref))
    own_copies += [pltpu.make_async_copy(src, dst, own_sem.at[3 + at]) for at, (src, dst) in enumerate(small)]
    for copy in own_copies[3:] + own_copies[:3]:
        copy.start()

    partners = [sib] + [chip(s, k) for s in (1, 3) for k in (j, other)]
    partners += [y_peer(s) for s in (1, 2, 3)] + [z_peer(s) for s in (1, 2, 3)]
    barrier = pltpu.get_barrier_semaphore()
    for partner in partners:
        pl.semaphore_signal(barrier, inc=1, device_id=partner, device_id_type=MESH)

    own_copies[3].wait()
    own_copies[4].wait()
    skel_t = jnp.where(lax.broadcasted_iota(jnp.int32, (ROWS, SKEL), 0) == skel_ref[...], 1.0, 0.0)
    scol[...] = jnp.broadcast_to(jnp.max(skel_t, axis=1, keepdims=True), (ROWS, 128))
    skel = jnp.transpose(skel_t)
    srow[...] = jnp.broadcast_to(jnp.sum(skel, axis=0, keepdims=True), (8, ROWS))
    chosen_t = jnp.where(
        lax.broadcasted_iota(jnp.int32, (SKEL, SKEL), 0) + gy * SKEL == urow_ref[...], 1.0, 0.0)
    chosen = jnp.transpose(chosen_t).astype(BF16)
    select = dot_nn(chosen, skel.astype(BF16)).astype(BF16)

    def prep(leaf):
        value = pts[leaf]
        high, low = split(value)
        hi[leaf] = high
        lo[leaf] = low
        wide = jnp.broadcast_to(jnp.sum(value * value, axis=1, keepdims=True) * BETA, (256, 128))
        ncol[leaf] = wide
        nrow[leaf] = jnp.transpose(wide)[0:8, :]

    for leaf in range(2):
        own_copies[leaf].wait()
        prep(leaf)

    rows_mine = jnp.zeros((SKEL, WIDTH), F32)
    for leaf in range(2):
        chosen_rows = select[:, 256 * leaf:256 * leaf + 256]
        rows_mine += dot_nn(chosen_rows, hi[leaf]) + dot_nn(chosen_rows, lo[leaf])
    for q in range(4):
        for h in range(2):
            contr[q, h] = rows_mine[64 * q + 32 * h:64 * q + 32 * h + 32, :]

    pl.semaphore_wait(barrier, len(partners))

    started = []

    def send(src, dst, device):
        at = len(started)
        copy = pltpu.make_async_remote_copy(
            src_ref=src, dst_ref=dst, send_sem=s_sem.at[at], recv_sem=r_sem.at[at],
            device_id=device, device_id_type=MESH)
        copy.start()
        started.append(copy)
        return copy

    def finish(copies):
        for copy in copies:
            copy.wait_recv()

    nodes = [gy, c * 2 + other, before * 2 + j, after * 2 + crossed]
    to_after, to_before = chip(1, j), chip(3, lax.rem(j + lax.div(before, 2), 2))

    bulk = {1: [], 3: []}

    def send_bulk(count=1):
        for _ in range(count):
            at = len(bulk[1])
            first, size = sum(CHUNKS[:at]), CHUNKS[at]
            leaf, rows = first // 256, pl.ds(first % 256, size)
            src = x_ref.at[pl.ds(first, size)]
            bulk[1].append(send(src, pts.at[4 + 2 * leaf, rows], to_after))
            bulk[3].append(send(src, pts.at[5 + 2 * leaf, rows], to_before))

    contr_msg = send(contr.at[:, other], contr_in, sib)
    label_msgs = [send(lab_ref, rt.at[slot, 0, 0:64], device)
                  for slot, device in ((2, to_after), (3, to_before), (1, sib))]
    send_bulk()
    sib_points = [send(x_ref.at[pl.ds(256 * leaf, 256)], pts.at[2 + leaf], sib) for leaf in range(2)]

    def many(parts, axis):
        return parts[0] if len(parts) == 1 else jnp.concatenate(parts, axis=axis)

    def affine(targets, sources):
        t_hi, t_lo, t_col = targets
        s_hi, s_lo, s_row = sources
        cross = dot_nt(t_hi, s_hi) + dot_nt(t_hi, s_lo) + dot_nt(t_lo, s_hi)
        wide = jnp.concatenate([t_col] * (s_hi.shape[0] // 128), axis=1)
        return jnp.exp2(cross * (2.0 * BETA) - wide - s_row)

    def as_targets(pieces):
        return (many([hi[l, f:f + n, :] for l, f, n in pieces], 0),
                many([lo[l, f:f + n, :] for l, f, n in pieces], 0),
                many([ncol[l, f:f + n, :] for l, f, n in pieces], 0))

    def as_sources(pieces):
        return (many([hi[l, f:f + n, :] for l, f, n in pieces], 0),
                many([lo[l, f:f + n, :] for l, f, n in pieces], 0),
                many([nrow[l, 0:1, f:f + n] for l, f, n in pieces], 1))

    def product_nt(k, rhs):
        k_hi, k_lo = split(k)
        r_hi, r_lo = split(rhs)
        both = dot_nt(k_hi, jnp.concatenate([r_hi, r_lo], axis=0))
        return both[:, :128] + both[:, 128:] + dot_nt(k_lo, r_hi)

    def product_nn(k_hi, k_lo, rhs):
        r_hi, r_lo = split(rhs)
        both = dot_nn(k_hi, jnp.concatenate([r_hi, r_lo], axis=1))
        return both[:, :128] + both[:, 128:] + dot_nn(k_lo, r_hi)

    lane = lax.broadcasted_iota(jnp.int32, (1, 128), 1)

    def pick(slot, row, at):
        return jnp.sum(jnp.where(lane == at, masks[slot, row:row + 1, :], 0.0), axis=1, keepdims=True)

    def near_rhs(slot, t, sources):
        return many([pick(slot, t, 2 * node + s) * rt[sl, 0, :, 256 * s + f:256 * s + f + n]
                     + pick(slot, 2, node) * rt[sl, 1, :, 256 * s + f:256 * s + f + n]
                     for sl, node, s, f, n in sources], 1)

    def near(target, slot, targets, source_pieces, source_terms):
        k = affine(as_targets([(l, f, n) for l, _, f, n in targets]), as_sources(source_pieces))
        at = 0
        for _, t, f, n in targets:
            acc[target, 256 * t + f:256 * t + f + n, :] += product_nt(
                k[at:at + n], near_rhs(slot, t, source_terms))
            at += n

    OWN = [(0, 0, 0, 256), (1, 1, 0, 256)]

    def up_sources(q, m):
        rows = pl.ds(pl.multiple_of((q * 4 + m) * 256, 256), 256)
        return uphi[rows, :], uplo[rows, :], upnrow[q * 4 + m, 0:1, :]

    def up_pair(parts):
        loaded = [up_sources(q, m) for q, m in parts]
        return (many([p[0] for p in loaded], 0), many([p[1] for p in loaded], 0), many([p[2] for p in loaded], 1))

    def up_rhs(slot, q, m):
        weights = upw[q, m]
        parts = []
        for n in range(4):
            cluster = n * 4 + m if q == 0 else m * 4 + n
            parts.append(weights[n].reshape(64, 128) * pick(slot, 3, cluster))
        return jnp.concatenate(parts, axis=0)

    acc[...] = jnp.zeros_like(acc)

    for slot in range(4):
        rt[slot, 0, 64:128, :] = jnp.where(
            lax.broadcasted_iota(jnp.int32, (64, ROWS), 0) == 0, 1.0, 0.0)
        rt[slot, 1, 72:128, :] = jnp.zeros((56, ROWS), F32)


    for copy in own_copies[5:]:
        copy.wait()
    def mask_row(entries):
        row = jnp.zeros((1, 128), F32)
        for entry in entries:
            row += jnp.where(lane == entry, 1.0, 0.0)
        return row

    for t in range(2):
        masks[0, t:t + 1, :] = mask_row([near_ref[t, e] - gx * 16 for e in range(8)])
    masks[0, 2:3, :] = mask_row([flocal_ref[0, e] for e in range(7)])
    masks[0, 3:4, :] = mask_row([fupper_ref[0, e] for e in range(15)])
    masks[0, 4:8, :] = jnp.zeros((4, 128), F32)
    mask_msgs = [send(masks.at[0], masks.at[slot], device)
                 for slot, device in ((1, sib), (2, to_after), (3, to_before))]

    def chip_sum(mine, incoming, total):
        for q in range(4):
            total[q] = mine[q, j] + incoming[q]

    def round_one(total, land):
        return [send(total.at[lax.rem(c + 3, 4)], land.at[0], chip(3, j)),
                send(total.at[lax.rem(c + 2, 4)], land.at[1], chip(1, j))]

    def round_two(total, land, middle, land_two):
        middle[0] = total[c] + land[0]
        middle[1] = total[after] + land[1]
        return [send(middle.at[0], land_two.at[1], chip(3, j)),
                send(middle.at[1], land_two.at[0], chip(1, j))]

    contr_msg.wait_recv()
    chip_sum(contr, contr_in, part)
    ones = round_one(part, land1)
    send_bulk()

    kown[...] = affine(as_targets([(0, 0, 256), (1, 0, 256)]), as_sources([(0, 0, 256), (1, 0, 256)]))
    own_copies[2].wait()
    inverse = 1.0 / jnp.sum(kown[...] * scol[:, 0:1], axis=0, keepdims=True)
    lower = product_nt(kown[...] * inverse, rt[0, 0]) * scol[...]

    finish(ones)
    twos = round_two(part, land1, mid, land2)
    send_bulk()

    rt[0, 1] = jnp.transpose(lower)

    rows_at = lax.broadcasted_iota(jnp.int32, (256, ROWS), 0)
    cols_at = lax.broadcasted_iota(jnp.int32, (256, ROWS), 1)
    for t in range(2):
        k = jnp.where(rows_at + 256 * t == cols_at, 0.0, kown[256 * t:256 * t + 256, :])
        acc[0, 256 * t:256 * t + 256, :] += product_nt(
            k, near_rhs(0, t, [(0, gy, 0, 0, 256), (0, gy, 1, 0, 256)]))

    finish(twos)
    quarter0 = mid[0] + land2[0]
    quarter1 = mid[1] + land2[1]
    uq[c, j] = quarter0
    uq[after, j] = quarter1
    up[0, z, y, j] = quarter0
    up[1, y, z, j] = quarter1
    threes = [send(uq.at[after, j], uq.at[after, j], chip(3, j)),
              send(uq.at[c, j], uq.at[c, j], chip(1, j))]

    def phase_one(buffer):
        return ([send(buffer.at[0, z, y, j], buffer.at[0, z, y, j], y_peer(s)) for s in (1, 3, 2)]
                + [send(buffer.at[1, y, z, j], buffer.at[1, y, z, j], z_peer(s)) for s in (1, 3, 2)])

    def phase_two(buffer):
        return {s: [send(buffer.at[0, z, :, j], buffer.at[0, z, :, j], z_peer(s)),
                    send(buffer.at[1, y, :, j], buffer.at[1, y, :, j], y_peer(s))] for s in (1, 3)}

    def pass_on(buffer):
        copies = []
        for step, rows in ((1, slice(0, 2)), (3, slice(2, 4))):
            m0, m1 = majors(step)
            copies += [send(buffer.at[0, m0, rows, j], buffer.at[0, m0, rows, j], z_peer(step)),
                       send(buffer.at[1, m1, rows, j], buffer.at[1, m1, rows, j], y_peer(step))]
        return copies

    def majors(step):
        return lax.rem(z + 4 - step, 4), lax.rem(y + 4 - step, 4)

    def share_step(buffer, step):
        m0, m1 = majors(step)
        return [send(buffer.at[0, m0, :, j], buffer.at[0, m0, :, j], sib),
                send(buffer.at[1, m1, :, j], buffer.at[1, m1, :, j], sib)]

    up_one = phase_one(up)
    send_bulk()
    weight_msgs = [send(rt.at[0, 1, 0:MSG], rt.at[slot, 1, 0:MSG], device)
                   for slot, device in ((1, sib), (2, to_after), (3, to_before))]

    send_bulk()

    finish(sib_points)
    label_msgs[2].wait_recv()
    mask_msgs[0].wait_recv()
    for leaf in range(2):
        prep(2 + leaf)

    finish(up_one)
    up_two = phase_two(up)
    up_share = {0: share_step(up, 0)}

    finish(threes)
    share = send(uq.at[:, j], uq.at[:, j], sib)
    weight_msgs[0].wait_recv()
    near(0, 0, OWN, [(2, 0, 256), (3, 0, 256)], [(1, nodes[1], 0, 0, 256), (1, nodes[1], 1, 0, 256)])
    send_bulk()
    share.wait_recv()

    value = uq[...].reshape(SKEL, WIDTH)
    u_hi, u_lo = split(value)
    u_col = jnp.broadcast_to(jnp.sum(value * value, axis=1, keepdims=True) * BETA, (SKEL, 128))
    k = affine((u_hi, u_lo, u_col), as_sources([(0, 0, 256), (1, 0, 256)]))
    total = jnp.sum(k, axis=0, keepdims=True)
    shares = k * jnp.where(srow[0:1, :] > 0.0, 1.0 / total, 0.0)
    partial_sum = product_nt(shares, rt[0, 1])
    for q in range(4):
        for h in range(2):
            wp[q, h] = partial_sum[64 * q + 32 * h:64 * q + 32 * h + 32, :]
    wp_msg = send(wp.at[:, other], wp_in, sib)

    def prep_up(q, m):
        value = up[q, m].reshape(256, WIDTH)
        rows = pl.ds(pl.multiple_of((q * 4 + m) * 256, 256), 256)
        high, low = split(value)
        uphi[rows, :] = high
        uplo[rows, :] = low
        wide = jnp.broadcast_to(jnp.sum(value * value, axis=1, keepdims=True) * BETA, (256, 128))
        upnrow[q * 4 + m] = jnp.transpose(wide)[0:8, :]

    def far_own(step):
        m0, m1 = majors(step)
        prep_up(0, m0)
        prep_up(1, m1)
        k_hi, k_lo = split(affine(as_targets([(0, 0, 256), (1, 0, 256)]), up_pair([(0, m0), (1, m1)])))
        kf_hi[step] = k_hi
        kf_lo[step] = k_lo

    wp_msg.wait_recv()
    chip_sum(wp, wp_in, wpart)
    w_ones = round_one(wpart, wland1)
    send_bulk()
    finish(up_share[0])
    far_own(0)
    finish(w_ones)
    w_twos = round_two(wpart, wland1, wmid, wland2)
    send_bulk(len(CHUNKS) - len(bulk[1]))
    for step in (1, 3):
        finish(up_two[step])
    up_two[2] = pass_on(up)
    for step in (1, 3):
        up_share[step] = share_step(up, step)

    taken = [0]

    def leaf_arrives(leaf):
        while taken[0] < len(CHUNKS) and sum(CHUNKS[:taken[0] + 1]) <= 256 * leaf + 256:
            bulk[1][taken[0]].wait_recv()
            bulk[3][taken[0]].wait_recv()
            taken[0] += 1
        for side in range(2):
            prep(4 + 2 * leaf + side)

    SIB = [(2, 0, 0, 256), (3, 1, 0, 256)]

    def from_leaf(target, slot, targets, leaf):
        near(target, slot, targets, [(4 + 2 * leaf, 0, 256), (5 + 2 * leaf, 0, 256)],
             [(2, nodes[2], leaf, 0, 256), (3, nodes[3], leaf, 0, 256)])

    finish(label_msgs[:2] + mask_msgs[1:] + weight_msgs[1:])
    leaf_arrives(0)
    from_leaf(3, 1, SIB, 0)
    finish(w_twos)
    upw[0, z, y, j] = wmid[0] + wland2[0]
    upw[1, y, z, j] = wmid[1] + wland2[1]
    w_up_one = phase_one(upw)
    from_leaf(0, 0, OWN, 0)

    finish(up_two[2])
    up_share[2] = share_step(up, 2)
    finish(up_share[1])
    far_own(1)
    finish(w_up_one)
    w_up_two = phase_two(upw)
    finish(up_share[3])
    far_own(3)
    for step in (1, 3):
        finish(w_up_two[step])
    w_pass = pass_on(upw)
    finish(up_share[2])
    far_own(2)
    finish(w_pass)
    w_share = [send(upw.at[:, :, :, j], upw.at[:, :, :, j], sib)]

    def far_kernel(leaf, q):
        return split(affine(as_targets([(leaf, 0, 256)]), up_pair([(q, m) for m in range(4)])))

    for side in range(2):
        kn_hi[side], kn_lo[side] = far_kernel(4 + side, 1 - side)

    finish(w_share)

    for step in range(4):
        m0, m1 = majors(step)
        rhs = jnp.concatenate([up_rhs(0, 0, m0), up_rhs(0, 1, m1)], axis=0)
        acc[0] += product_nn(kf_hi[step], kf_lo[step], rhs)

    def far_terms(side):
        return jnp.concatenate([up_rhs(2 + side, 1 - side, m) for m in range(4)], axis=0)

    for side in range(2):
        acc[1 + side, 0:256, :] += product_nn(kn_hi[side], kn_lo[side], far_terms(side))

    leaf_arrives(1)
    both = [[(4 + side, 0, 256), (6 + side, 0, 256)] for side in range(2)]
    terms = [[(2 + side, nodes[2 + side], leaf, 0, 256) for leaf in range(2)] for side in range(2)]
    k_hi, k_lo = split(affine(as_targets(both[0]), as_sources(both[1])))
    turned = []
    for t in range(2):
        cols = slice(256 * t, 256 * t + 256)
        r_hi, r_lo = split(near_rhs(3, t, terms[0]))
        two = dot_nn(jnp.concatenate([r_hi, r_lo], axis=0), k_hi[:, cols])
        turned.append(two[:128] + two[128:] + dot_nn(r_hi, k_lo[:, cols]))
        rows = slice(256 * t, 256 * t + 256)
        r_hi, r_lo = split(near_rhs(2, t, terms[1]))
        two = dot_nt(k_hi[rows], jnp.concatenate([r_hi, r_lo], axis=0))
        acc[1, rows, :] += two[:, :128] + two[:, 128:] + dot_nt(k_lo[rows], r_hi)
    ret_out[1] = jnp.concatenate(turned, axis=1)
    backs = []
    for side in range(2):
        f_hi, f_lo = far_kernel(6 + side, 1 - side)
        acc[1 + side, 256:512, :] += product_nn(f_hi, f_lo, far_terms(side))
        done = jnp.transpose(acc[1 + side])
        ret_out[side] = done if side == 0 else ret_out[1] + done
        backs.append(send(ret_out.at[side, 0:MSG], ret_in.at[side, 0:MSG],
                          chip(3, j) if side == 0 else chip(1, crossed)))
    from_leaf(3, 1, SIB, 1)
    ret_out[2] = jnp.transpose(acc[3])
    backs.append(send(ret_out.at[2, 0:MSG], ret_in.at[2, 0:MSG], sib))
    from_leaf(0, 0, OWN, 1)
    sums = jnp.transpose(acc[0])[0:MSG]
    for side in (2, 0, 1):
        backs[side].wait_recv()
        sums += ret_in[side, 0:MSG]
    out_ref[...] = sums[0:LABELS] / sums[LABELS:LABELS + 1]

    for copy in started:
        copy.wait_send()


N_COPIES = 110


def on_device(points, labels, skeleton_rows, upper_rows, near_list, far_local, far_upper):
    vmem = pl.BlockSpec(memory_space=pltpu.VMEM)
    hbm = pl.BlockSpec(memory_space=pl.ANY)
    result = pl.pallas_call(
        kernel,
        out_shape=jax.ShapeDtypeStruct((LABELS, ROWS), F32),
        in_specs=[hbm] * 7,
        out_specs=vmem,
        scratch_shapes=[
            pltpu.VMEM(skeleton_rows.shape, jnp.int32),
            pltpu.VMEM(upper_rows.shape, jnp.int32),
            pltpu.SMEM(near_list.shape, jnp.int32),
            pltpu.SMEM(far_local.shape, jnp.int32),
            pltpu.SMEM(far_upper.shape, jnp.int32),
            pltpu.VMEM((8, LEAF, WIDTH), F32),
            pltpu.VMEM((8, LEAF, WIDTH), BF16),
            pltpu.VMEM((8, LEAF, WIDTH), BF16),
            pltpu.VMEM((8, LEAF, 128), F32),
            pltpu.VMEM((8, 8, LEAF), F32),
            pltpu.VMEM((4, 2, 128, ROWS), F32),
            pltpu.VMEM((4, 8, 128), F32),
            pltpu.VMEM((ROWS, ROWS), F32),
            pltpu.VMEM((ROWS, 128), F32),
            pltpu.VMEM((8, ROWS), F32),
            pltpu.VMEM((4, 2, 32, WIDTH), F32),
            pltpu.VMEM((4, 32, WIDTH), F32),
            pltpu.VMEM((4, 32, WIDTH), F32),
            pltpu.VMEM((2, 32, WIDTH), F32),
            pltpu.VMEM((2, 32, WIDTH), F32),
            pltpu.VMEM((2, 32, WIDTH), F32),
            pltpu.VMEM((4, 2, 32, WIDTH), F32),
            pltpu.VMEM((2, 4, 4, 2, 32, WIDTH), F32),
            pltpu.VMEM((2048, WIDTH), BF16),
            pltpu.VMEM((2048, WIDTH), BF16),
            pltpu.VMEM((8, 8, 256), F32),
            pltpu.VMEM((4, 2, 32, 128), F32),
            pltpu.VMEM((4, 32, 128), F32),
            pltpu.VMEM((4, 32, 128), F32),
            pltpu.VMEM((2, 32, 128), F32),
            pltpu.VMEM((2, 32, 128), F32),
            pltpu.VMEM((2, 32, 128), F32),
            pltpu.VMEM((2, 4, 4, 2, 32, 128), F32),
            pltpu.VMEM((4, ROWS, ROWS), BF16),
            pltpu.VMEM((4, ROWS, ROWS), BF16),
            pltpu.VMEM((2, LEAF, 1024), BF16),
            pltpu.VMEM((2, LEAF, 1024), BF16),
            pltpu.VMEM((4, ROWS, 128), F32),
            pltpu.VMEM((3, 128, ROWS), F32),
            pltpu.VMEM((3, 128, ROWS), F32),
            pltpu.SemaphoreType.DMA((8,)),
            pltpu.SemaphoreType.DMA((N_COPIES,)),
            pltpu.SemaphoreType.DMA((N_COPIES,)),
        ],
        compiler_params=pltpu.CompilerParams(
            collective_id=0, has_side_effects=True, vmem_limit_bytes=62 * 1024 * 1024),
        cost_estimate=pl.CostEstimate(
            flops=64 * 6 * 256 * 256 * 768, bytes_accessed=2 * 1024 * 1024, transcendentals=64 * 256 * 256),
    )(points, labels.T, skeleton_rows, upper_rows, near_list, far_local, far_upper)
    return result.T


def solution(mesh):
    return jax.shard_map(
        on_device,
        mesh=mesh,
        in_specs=(
            P(("gx", "gy"), None),
            P(("gx", "gy"), None),
            P(("gx", "gy"), None),
            P("gx", None),
            P(("gx", "gy"), None),
            P(("gx", "gy"), None),
            P(("gx", "gy"), None),
        ),
        out_specs=P(("gx", "gy"), None),
        check_vma=False,
    )
```
